256 devices in a mesh: dp: 16 (over x, y), tensor: 16 (over z, core).
Axes of the slice: x: 4, y: 4, z: 8, core: 2. Of those that a mesh axis runs over, the one named last changes fastest.
Arguments:
- activations: bfloat16 [4096, 16384], P('dp', 'tensor'), may hold values from -6 to 6
- angles: float32 [14, 8192], P(None, 'tensor'), may hold values from -3.140625 to 3.140625
- clip_bits: int32 [256, 16384], P('dp', 'tensor'), may hold values from 0 to 65535, as said below
- codes: bfloat16 [16384, 10240], P('tensor', 'dp'), may hold values from -127 to 127, as said below
- exponents: int32 [10240], replicated, may hold values from -16 to -13
- cotangent: bfloat16 [4096, 10240], P('dp', 'tensor'), may hold values from -6 to 6
Outputs:
- input_grad: bfloat16 [4096, 16384], P('dp', 'tensor')
- angle_grad: float32 [14, 8192], P(None, 'tensor')
The draws below stay inside these ranges and needn't reach their ends.
Inputs may be any that keep to these rules, and one draw needn't show every extreme that they name: Bit k (0 to 15) of clip_bits[w, i] is the clip mask of token 16 w + k at feature i; higher bits are zero. `codes`: every entry is a whole number.
All inputs are finite; a program needn't handle non-finite values.
Results may differ from the reference program's by a relative error of at most 0.003.
Values may be sent and summed in bfloat16 or wider, within the bound.
A program may use at most 128 MiB of HBM per device.

```python
import jax
import jax.numpy as jnp
from jax import lax

D = 16384
OUT = 10240
SECTIONS = 14
TOK_DEV = 256
TOKENS = 4096


def draw_clip_bits(key, part):
    shape = (TOKENS // 16, D)

    def add_bit(k, total):
        level = jax.random.randint(jax.random.fold_in(key, k), shape, 0, 8)
        bit = jnp.where(level != 0, 1, 0).astype(jnp.int32)
        return total + jnp.left_shift(bit, k)
    total = lax.fori_loop(0, 16, add_bit, jnp.zeros(shape, jnp.int32))
    return total.at[0, :].set(65535)


def draw_codes(key, part):
    first = jax.random.fold_in(key, 11)
    second = jax.random.fold_in(key, 12)
    values = jax.random.randint(first, (D, OUT), -64, 64) + jax.random.randint(second, (D, OUT), -63, 64)
    return values.astype(jnp.float32).astype(jnp.bfloat16)


def set_ends(array, key, smallest, top_value):
    shape = array.shape
    index_at = [jax.random.randint(jax.random.fold_in(key, axis), (), 0, shape[axis]) for axis in range(len(shape))]
    array = array.at[tuple(index_at)].set(smallest)
    longest = shape.index(max(shape))
    index_at[longest] = (index_at[longest] + 1) % shape[longest]
    return array.at[tuple(index_at)].set(top_value)


def block_scale(stream_key, dims, split, smallest, top_value):
    gain = 1.0
    for position, shards_of in split:
        steps = jax.random.uniform(jax.random.fold_in(jax.random.fold_in(stream_key, 6), position), (shards_of,), jnp.float32, smallest / len(split), top_value / len(split))
        gain = gain * jnp.repeat(jnp.exp(steps), dims[position] // shards_of).reshape((-1,) + (1,) * (len(dims) - 1 - position))
    return gain


def bell_draw(stream_key, shape, scale, most, split=(), held_as=jnp.bfloat16):
    gain = block_scale(stream_key, shape, split, -0.22, 0.18) if split else 1.0
    values = jax.random.normal(stream_key, shape, jnp.float32) * scale * gain
    return jnp.minimum(jnp.maximum(values, -most), most).astype(held_as)


def setup_inputs(seed: int = 0) -> dict:
    seeds = jax.random.split(jax.random.key(seed), 7)
    activations = bell_draw(seeds[0], (TOKENS, D), 1.0, 6.0, ((0, 16), (1, 16)))
    angles = jnp.clip(jax.random.uniform(seeds[1], (SECTIONS, D // 2), jnp.float32, -3.140625, 3.140625), -3.140625, 3.140625)
    clip_bits = draw_clip_bits(jax.random.fold_in(seeds[6], 71), 0)
    codes = draw_codes(jax.random.fold_in(seeds[6], 71), 0)
    exponents = set_ends(jax.random.randint(seeds[4], (OUT,), -16, -12), jax.random.fold_in(seeds[4], 1), -16, (-12) - 1).astype(jnp.int32)
    cotangent = bell_draw(seeds[5], (TOKENS, OUT), 1.0, 6.0, ((0, 16), (1, 16)))
    return dict(activations=activations, angles=angles, clip_bits=clip_bits, codes=codes, exponents=exponents, cotangent=cotangent)


def unpack_mask(words, rows):
    shifts = jnp.arange(16, dtype=jnp.int32)
    bits = jnp.bitwise_and(jnp.right_shift(words[:, None, :], shifts[None, :, None]), 1)
    return bits.reshape(rows, words.shape[1]).astype(jnp.float32)


def split_pairs(field, angle_row, section):
    rows, width = field.shape
    half = 2 ** section
    shaped = field.reshape(rows, width // (2 * half), 2, half)
    theta = angle_row.reshape(width // (2 * half), half)
    return jnp.cos(theta), jnp.sin(theta), shaped[:, :, 0, :], shaped[:, :, 1, :]


def forward_section(field, angle_row, section):
    cosine, sine, lower, upper = split_pairs(field, angle_row, section)
    new_lower = cosine * lower - sine * upper
    new_upper = sine * lower + cosine * upper
    return jnp.stack([new_lower, new_upper], axis=2).reshape(field.shape)


def block_pass(acts, words, cots, weight, angles):
    rows = acts.shape[0]
    passed = unpack_mask(words, rows)
    projected = lax.dot_general(cots, weight, (((1,), (1,)), ((), ())), preferred_element_type=jnp.float32)
    grad = projected * passed
    states = [acts.astype(jnp.float32)]
    for section in range(SECTIONS):
        states.append(forward_section(states[-1], angles[section], section))
    terms = [None] * SECTIONS
    for section in reversed(range(SECTIONS)):
        cosine, sine, out_lower, out_upper = split_pairs(states[section + 1], angles[section], section)
        unused_c, unused_s, grad_lower, grad_upper = split_pairs(grad, angles[section], section)
        terms[section] = jnp.sum(grad_upper * out_lower - grad_lower * out_upper, axis=0).reshape(-1)
        prev_lower = cosine * grad_lower + sine * grad_upper
        prev_upper = cosine * grad_upper - sine * grad_lower
        grad = jnp.stack([prev_lower, prev_upper], axis=2).reshape(grad.shape)
    return grad.astype(jnp.bfloat16), jnp.stack(terms)


def reference(activations, angles, clip_bits, codes, exponents, cotangent):
    scale = jnp.exp2(exponents.astype(jnp.float32))
    weight = (codes.astype(jnp.float32) * scale[None, :]).astype(jnp.bfloat16)
    blocks = TOKENS // TOK_DEV
    acts = activations.reshape(blocks, TOK_DEV, D)
    words = clip_bits.reshape(blocks, TOK_DEV // 16, D)
    cots = cotangent.reshape(blocks, TOK_DEV, OUT)

    def step(total, items):
        grad, terms = block_pass(items[0], items[1], items[2], weight, angles)
        return total + terms, grad

    total, grads = lax.scan(step, jnp.zeros((SECTIONS, D // 2), jnp.float32), (acts, words, cots))
    return grads.reshape(TOKENS, D), total
```

```python
import jax
import jax.numpy as jnp
from jax import lax
from jax.experimental import pallas as pl
from jax.experimental.pallas import tpu as pltpu
from jax.sharding import PartitionSpec as P

MESH = pl.DeviceIdType.MESH
F32 = jnp.float32
BF16 = jnp.bfloat16
CHUNK = 256
CHUNKS = 4


def place():
    d = lax.axis_index("dp")
    k = lax.axis_index("tensor")
    return d, k, d // 4, d % 4, k // 2, k % 2


def remote(src, dst, send, recv, to):
    return pltpu.make_async_remote_copy(
        src_ref=src, dst_ref=dst, send_sem=send, recv_sem=recv, device_id=to, device_id_type=MESH
    )


def project_kernel(
    acts, clip, codes, exps, cot, angles,
    q_out, a_out, ang_out,
    scaled, cots, w_left, w_right, w_far, sent, got, whole,
    x_send, wl_sem, wr_sem, wf_sem, b_send, b_recv, z_send, up_sem, down_sem, sib_sem,
    d_send, d_recv, e_send, e_recv, f_send, f_recv, g_send, g_recv, h_send, h_recv,
):
    d, k, x, y, z, c = place()
    slot = c * 8 + z

    def dev(px, py, pz, pc):
        return (px * 4 + py, pz * 2 + pc)

    right = dev((x + 1) % 4, y, z, c)
    left = dev((x + 3) % 4, y, z, c)
    up = dev(x, y, (z + 1) % 8, c)
    down = dev(x, y, (z + 7) % 8, c)
    sibling = dev(x, y, z, 1 - c)

    barrier = pltpu.get_barrier_semaphore()

    def greet(to):
        pl.semaphore_signal(barrier, inc=1, device_id=to, device_id_type=MESH)

    greet(right)
    greet(left)
    for step in range(1, 4):
        for core in range(2):
            greet(dev(x, (y + step) % 4, z, core))

    @pl.loop(1, 16)
    def _(i):
        greet((d, (k + i) % 16))

    pl.semaphore_wait(barrier, 23)

    for f in range(CHUNKS):
        rows = pl.ds(f * CHUNK, CHUNK)
        remote(codes.at[rows], w_left.at[rows], x_send.at[0], wl_sem.at[f], right).start()
        remote(codes.at[rows], w_right.at[rows], x_send.at[1], wr_sem.at[f], left).start()

    minus = -exps[:, pl.ds(pl.multiple_of(k * 640, 128), 640)]
    scale = jnp.ones((1, 640), F32)
    for bit in range(5):
        on = jnp.bitwise_and(jnp.right_shift(minus, bit), 1) == 1
        scale = jnp.where(on, scale * (2.0 ** -(2**bit)), scale)
    scaled[...] = (cot[...].astype(F32) * scale).astype(BF16)

    def piece(part, token_group, half):
        start = pl.multiple_of(token_group * 256 + half * 128, 128)
        return cots.at[part, pl.ds(start, 128), :]

    owner_y = k % 4
    for half in range(2):
        mine = jnp.logical_and(owner_y == y, c == half)

        @pl.when(mine)
        def _():
            start = pl.multiple_of(y * 256 + half * 128, 128)
            cots[z // 2, pl.ds(start, 128), :] = scaled[half * 128 : (half + 1) * 128, :]

        @pl.when(jnp.logical_not(mine))
        def _():
            remote(
                scaled.at[pl.ds(half * 128, 128), :],
                piece(z // 2, y, half),
                b_send.at[half],
                b_recv.at[y],
                dev(x, owner_y, z, half),
            ).start()

    ang_out[c, z, 0:14, :] = angles[...]
    ang_out[c, z, 14:16, :] = jnp.zeros((2, 512), F32)

    @pl.loop(1, 8)
    def _(i):
        remote(
            ang_out.at[c, z], ang_out.at[c, z], g_send, g_recv, (d, ((z + i) % 8) * 2 + c)
        ).start()

    def to_sibling(ref):
        remote(ref, ref, z_send.at[2], sib_sem, sibling).start()

    is_source = (z % 2) == (y // 2)

    @pl.when(is_source)
    def _():
        for g in range(4):
            ref = piece(z // 2, g, c)

            @pl.when(jnp.logical_not(jnp.logical_and(y == g, y % 2 == c)))
            def _():
                remote(ref, ref, b_send.at[0], b_recv.at[g], sibling).wait_recv()

            remote(ref, ref, z_send.at[0], up_sem.at[0, g], up).start()
            remote(ref, ref, z_send.at[1], down_sem.at[0, g], down).start()
            to_sibling(ref)

    def pass_on(t):
        below = (z + 8 - t) % 8
        above = (z + t) % 8

        @pl.when((below % 2) == (y // 2))
        def _():
            for g in range(4):
                if t < 4 or g < 2:
                    ref = piece(below // 2, g, c)
                    remote(ref, ref, z_send.at[0], up_sem.at[t - 1, g], up).wait_recv()
                    if t < 3 or (t == 3 and g < 2):
                        remote(ref, ref, z_send.at[0], up_sem.at[t, g], up).start()
                    to_sibling(ref)
                if t < 4 or g >= 2:
                    ref = piece(above // 2, g, c)
                    remote(ref, ref, z_send.at[1], down_sem.at[t - 1, g], down).wait_recv()
                    if t < 3 or (t == 3 and g >= 2):
                        remote(ref, ref, z_send.at[1], down_sem.at[t, g], down).start()
                    to_sibling(ref)

    def forward(f):
        rows = pl.ds(f * CHUNK, CHUNK)
        if f % 2 == 0:
            remote(w_left.at[rows], w_left.at[rows], x_send.at[0], wl_sem.at[f], right).wait_recv()
            remote(w_left.at[rows], w_far.at[rows], x_send.at[2], wf_sem.at[f], right).start()
        else:
            remote(w_right.at[rows], w_right.at[rows], x_send.at[1], wr_sem.at[f], left).wait_recv()
            remote(w_right.at[rows], w_far.at[rows], x_send.at[3], wf_sem.at[f], left).start()

    pass_on(1)
    pass_on(2)
    forward(0)
    forward(1)
    pass_on(3)
    pass_on(4)
    forward(2)
    forward(3)

    mine16 = pl.ds(pl.multiple_of(slot * 16, 16), 16)

    @pl.loop(1, 16)
    def _(i):
        to = (k + i) % 16
        remote(
            acts.at[pl.ds(pl.multiple_of(to * 16, 16), 16), :],
            a_out.at[mine16, :],
            f_send,
            f_recv,
            (d, to),
        ).start()

    own16 = pl.ds(pl.multiple_of(k * 16, 16), 16)
    a_out[mine16, :] = acts[own16, :]

    remote(ang_out.at[0, 0:7], ang_out.at[0, 0:7], g_send, g_recv, sibling).wait_recv()
    remote(ang_out.at[c], ang_out.at[c], h_send, h_recv, sibling).start()

    remote(cots.at[0:2], cots.at[0:2], z_send.at[2], sib_sem, sibling).wait_recv()

    def finish(f):
        lanes = pl.ds(pl.multiple_of(f * CHUNK, CHUNK), CHUNK)
        remote(got.at[f], got.at[f], d_send, d_recv.at[f], sibling).wait_recv()
        place_in_word = lax.broadcasted_iota(jnp.int32, (16, CHUNK), 0)

        def masked(w):
            rows = pl.ds(pl.multiple_of(w * 16, 16), 16)
            total = whole[f, rows, :]
            for j in range(3):
                total = total + got[f, j, rows, :].astype(F32)
            word = jnp.broadcast_to(clip[pl.ds(w, 1), lanes], (16, CHUNK))
            bit = jnp.bitwise_and(jnp.right_shift(word, place_in_word), 1)
            return rows, jnp.where(bit == 1, total, 0.0)

        @pl.loop(1, 16)
        def _(i):
            to = (k + i) % 16
            rows, value = masked(to)
            whole[f, rows, :] = value
            remote(
                whole.at[f, rows, :], q_out.at[mine16, lanes], e_send, e_recv, (d, to)
            ).start()

        _, value = masked(k)
        q_out[mine16, lanes] = value

    @pl.loop(0, 4 * CHUNKS)
    def _(i):
        f = i // 4
        j = i % 4
        to_y = (y + j + 1) % 4
        rows = pl.ds(pl.multiple_of(f * CHUNK, CHUNK), CHUNK)
        tokens = pl.ds(pl.multiple_of(to_y * 256, 256), 256)

        @pl.when(j == 0)
        def _():
            @pl.when(f % 2 == 1)
            def _():
                remote(w_left.at[rows], w_left.at[rows], x_send.at[0], wl_sem.at[f], right).wait_recv()

            @pl.when(f % 2 == 0)
            def _():
                remote(w_right.at[rows], w_right.at[rows], x_send.at[1], wr_sem.at[f], left).wait_recv()

            remote(w_far.at[rows], w_far.at[rows], x_send.at[2], wf_sem.at[f], right).wait_recv()

        def product(part, ref):
            return lax.dot_general(
                cots[part, tokens, :], ref[rows, :], (((1,), (1,)), ((), ())),
                preferred_element_type=F32,
            )

        total = product(x, codes)
        total = total + product((x + 3) % 4, w_left)
        total = total + product((x + 1) % 4, w_right)
        total = total + product((x + 2) % 4, w_far)

        @pl.when(j < 3)
        def _():
            sent[f, j] = total.astype(BF16)
            remote(
                sent.at[f, j], got.at[f, j], d_send, d_recv.at[f], dev(x, to_y, z, c)
            ).start()

        @pl.when(j == 3)
        def _():
            whole[f] = total

            @pl.when(f > 0)
            def _():
                finish(f - 1)

    finish(CHUNKS - 1)

    remote(q_out.at[0:240], q_out.at[0:240], e_send, e_recv, sibling).wait()
    remote(a_out.at[0:240], a_out.at[0:240], f_send, f_recv, sibling).wait()
    remote(ang_out.at[0, 0:7], ang_out.at[0, 0:7], g_send, g_recv, sibling).wait_send()
    remote(ang_out.at[0], ang_out.at[0], h_send, h_recv, sibling).wait()
    remote(sent, got, d_send, d_recv.at[0], sibling).wait_send()
    remote(codes, w_left, x_send.at[0], wl_sem.at[0], right).wait_send()
    remote(codes, w_right, x_send.at[1], wr_sem.at[0], left).wait_send()
    half_rows = pl.ds(0, 512)
    remote(w_left.at[half_rows], w_far.at[half_rows], x_send.at[2], wf_sem.at[0], right).wait_send()
    remote(w_left.at[half_rows], w_far.at[half_rows], x_send.at[3], wf_sem.at[0], left).wait_send()
    for half in range(2):
        @pl.when(jnp.logical_not(jnp.logical_and(owner_y == y, c == half)))
        def _():
            ref = scaled.at[pl.ds(half * 128, 128), :]
            remote(ref, ref, b_send.at[half], b_recv.at[0], sibling).wait_send()
    for way in range(2):
        @pl.when(is_source)
        def _():
            remote(cots.at[0], cots.at[0], z_send.at[way], sib_sem, sibling).wait_send()

        @pl.when(jnp.logical_not(is_source))
        def _():
            ref = cots.at[0, 0:768, :]
            remote(ref, ref, z_send.at[way], sib_sem, sibling).wait_send()
    remote(cots.at[0:2], cots.at[0:2], z_send.at[2], sib_sem, sibling).wait_send()


VMEM = pl.BlockSpec(memory_space=pltpu.VMEM)


def project(acts, clip, codes, exps, cot, angles):
    dma = pltpu.SemaphoreType.DMA
    return pl.pallas_call(
        project_kernel,
        out_shape=(
            jax.ShapeDtypeStruct((256, 1024), F32),
            jax.ShapeDtypeStruct((256, 1024), BF16),
            jax.ShapeDtypeStruct((2, 8, 16, 512), F32),
        ),
        in_specs=[VMEM] * 6,
        out_specs=(VMEM,) * 3,
        scratch_shapes=[
            pltpu.VMEM((256, 640), BF16),
            pltpu.VMEM((4, 1024, 640), BF16),
            pltpu.VMEM((1024, 640), BF16),
            pltpu.VMEM((1024, 640), BF16),
            pltpu.VMEM((1024, 640), BF16),
            pltpu.VMEM((CHUNKS, 3, 256, CHUNK), BF16),
            pltpu.VMEM((CHUNKS, 3, 256, CHUNK), BF16),
            pltpu.VMEM((CHUNKS, 256, CHUNK), F32),
            dma((4,)), dma((CHUNKS,)), dma((CHUNKS,)), dma((CHUNKS,)),
            dma((2,)), dma((4,)), dma((3,)), dma((4, 4)), dma((4, 4)), dma,
            dma, dma((CHUNKS,)), dma, dma, dma, dma, dma, dma, dma, dma,
        ],
        compiler_params=pltpu.CompilerParams(
            collective_id=0, has_side_effects=True, vmem_limit_bytes=48 * 2**20
        ),
        cost_estimate=pl.CostEstimate(flops=5400000000, bytes_accessed=6000000, transcendentals=0),
    )(acts, clip, codes, exps, cot, angles)


def sine_cosine(theta):
    h = theta * 0.5
    u = h * h
    s = 1.0 / 6227020800.0
    for term in (-1.0 / 39916800.0, 1.0 / 362880.0, -1.0 / 5040.0, 1.0 / 120.0, -1.0 / 6.0, 1.0):
        s = s * u + term
    s = s * h
    c = -1.0 / 87178291200.0
    for term in (1.0 / 479001600.0, -1.0 / 3628800.0, 1.0 / 40320.0, -1.0 / 720.0, 1.0 / 24.0, -0.5, 1.0):
        c = c * u + term
    return 2.0 * s * c, 1.0 - 2.0 * s * s


def squeezed(index, section):
    low = (1 << section) - 1
    return jnp.left_shift(jnp.right_shift(index, section + 1), section) | (index & low)


def lane_partner(value, section):
    lanes = lax.broadcasted_iota(jnp.int32, value.shape, 1)
    return jnp.take_along_axis(value, lanes ^ (1 << section), axis=1, mode="promise_in_bounds")


def pair_bit(section):
    return 8 if section == 10 else 1 << (section - 11)


def pairs_of(section):
    bit = pair_bit(section)
    pairs = []
    for m in range(8):
        b = section - 10
        lower = ((m >> b) << (b + 1)) | (m & ((1 << b) - 1))
        s0 = (lower % 2) * 8 + lower // 2
        pairs.append((m, s0, s0 + bit))
    return pairs


def butterfly_kernel(q_in, a_in, ang, q_out, g_out, cos_t, sin_t, states, terms, tall):
    lane_row = lax.broadcasted_iota(jnp.int32, (128, 128), 1)
    lane_col = lax.broadcasted_iota(jnp.int32, (128, 128), 0)
    for s in range(7):
        rows = jnp.concatenate(
            [ang[core, :, s, a * 128 : (a + 1) * 128] for a in range(4) for core in range(2)], axis=0
        )
        for b in range(2):
            pick = jnp.where(lane_col == b * 64 + squeezed(lane_row, s), 1.0, 0.0)
            theta = jnp.dot(rows, pick, precision=lax.Precision.HIGHEST, preferred_element_type=F32)
            sine, cosine = sine_cosine(theta)
            upper = (lax.broadcasted_iota(jnp.int32, theta.shape, 1) & (1 << s)) != 0
            signed = jnp.where(upper, sine, -sine)
            for a in range(4):
                cos_t[s, 2 * a + b] = cosine[a * 16 : (a + 1) * 16]
                sin_t[s, 2 * a + b] = signed[a * 16 : (a + 1) * 16]
    for s in range(7, 14):
        for a in range(4):
            for core in range(2):
                sine, cosine = sine_cosine(ang[core, :, s, a * 128 : (a + 1) * 128])
                cos_t[s, a, core * 8 : core * 8 + 8] = cosine
                sin_t[s, a, core * 8 : core * 8 + 8] = sine

    def row(table, s, tile, index):
        return jnp.broadcast_to(table[s, tile, pl.ds(index, 1), :], (16, 128))

    @pl.loop(0, 16)
    def _(kk):
        rows = pl.ds(pl.multiple_of(kk * 16, 16), 16)
        field = [a_in[rows, t * 128 : (t + 1) * 128].astype(F32) for t in range(8)]
        for s in range(7):
            for t in range(8):
                field[t] = row(cos_t, s, t, kk) * field[t] + row(sin_t, s, t, kk) * lane_partner(field[t], s)
                states[s, rows, t * 128 : (t + 1) * 128] = field[t]
        for s in range(7, 10):
            b = s - 7
            for a in range(4):
                lo = ((a >> b) << (b + 1)) | (a & ((1 << b) - 1))
                hi = lo + (1 << b)
                cosine, sine = row(cos_t, s, a, kk), row(sin_t, s, a, kk)
                field[lo], field[hi] = (
                    cosine * field[lo] - sine * field[hi],
                    sine * field[lo] + cosine * field[hi],
                )
            for t in range(8):
                states[s, rows, t * 128 : (t + 1) * 128] = field[t]

    for t in range(8):
        lanes = slice(t * 128, (t + 1) * 128)

        def fixed_row(table, s, m):
            return jnp.broadcast_to(
                table[s, t % 4, (t // 4) * 8 + m : (t // 4) * 8 + m + 1, :], (8, 128)
            )

        for s in range(10, 14):
            for m, lo, hi in pairs_of(s):
                cosine, sine = fixed_row(cos_t, s, m), fixed_row(sin_t, s, m)
                for half in range(2):
                    lo_rows = slice(lo * 16 + half * 8, lo * 16 + half * 8 + 8)
                    hi_rows = slice(hi * 16 + half * 8, hi * 16 + half * 8 + 8)
                    v_lo, v_hi = states[s - 1, lo_rows, lanes], states[s - 1, hi_rows, lanes]
                    states[s, lo_rows, lanes] = cosine * v_lo - sine * v_hi
                    states[s, hi_rows, lanes] = sine * v_lo + cosine * v_hi
        for s in (13, 12, 11, 10):
            source = q_in if s == 13 else tall
            for m, lo, hi in pairs_of(s):
                cosine, sine = fixed_row(cos_t, s, m), fixed_row(sin_t, s, m)
                total = None
                for half in range(2):
                    lo_rows = slice(lo * 16 + half * 8, lo * 16 + half * 8 + 8)
                    hi_rows = slice(hi * 16 + half * 8, hi * 16 + half * 8 + 8)
                    q_lo, q_hi = source[lo_rows, lanes], source[hi_rows, lanes]
                    term = q_hi * states[s, lo_rows, lanes] - q_lo * states[s, hi_rows, lanes]
                    total = term if total is None else total + term
                    tall[lo_rows, lanes] = cosine * q_lo + sine * q_hi
                    tall[hi_rows, lanes] = cosine * q_hi - sine * q_lo
                g_out[(t // 4) * 8 + m, s, (t % 4) * 128 : (t % 4 + 1) * 128] = jnp.sum(total, axis=0)

    @pl.loop(0, 16)
    def _(kk):
        rows = pl.ds(pl.multiple_of(kk * 16, 16), 16)
        grad = [tall[rows, t * 128 : (t + 1) * 128] for t in range(8)]
        for s in (9, 8, 7):
            b = s - 7
            for a in range(4):
                lo = ((a >> b) << (b + 1)) | (a & ((1 << b) - 1))
                hi = lo + (1 << b)
                cosine, sine = row(cos_t, s, a, kk), row(sin_t, s, a, kk)
                term = grad[hi] * states[s, rows, lo * 128 : (lo + 1) * 128]
                term = term - grad[lo] * states[s, rows, hi * 128 : (hi + 1) * 128]
                g_out[kk, s, a * 128 : (a + 1) * 128] = jnp.sum(term, axis=0)
                grad[lo], grad[hi] = (
                    cosine * grad[lo] + sine * grad[hi],
                    cosine * grad[hi] - sine * grad[lo],
                )
        for s in (6, 5, 4, 3, 2, 1, 0):
            for t in range(8):
                other = lane_partner(grad[t], s)
                term = other * states[s, rows, t * 128 : (t + 1) * 128]
                terms[s, t, pl.ds(kk, 1), :] = jnp.sum(term, axis=0, keepdims=True)
                grad[t] = row(cos_t, s, t, kk) * grad[t] - row(sin_t, s, t, kk) * other
        for t in range(8):
            q_out[rows, t * 128 : (t + 1) * 128] = grad[t].astype(BF16)

    for s in range(7):
        sign = jnp.where((lane_col & (1 << s)) == 0, 1.0, -1.0)
        for a in range(4):
            total = None
            for b in range(2):
                pick = jnp.where(lane_row == b * 64 + squeezed(lane_col, s), sign, 0.0)
                part = jnp.dot(
                    terms[s, 2 * a + b], pick, precision=lax.Precision.HIGHEST, preferred_element_type=F32
                )
                total = part if total is None else total + part
            g_out[:, s, a * 128 : (a + 1) * 128] = total
    g_out[:, 14:16, :] = jnp.zeros((16, 2, 512), F32)


def butterfly(grad, acts, ang):
    return pl.pallas_call(
        butterfly_kernel,
        out_shape=(
            jax.ShapeDtypeStruct((256, 1024), BF16),
            jax.ShapeDtypeStruct((16, 16, 512), F32),
        ),
        in_specs=[VMEM] * 3,
        out_specs=(VMEM,) * 2,
        scratch_shapes=[
            pltpu.VMEM((14, 8, 16, 128), F32),
            pltpu.VMEM((14, 8, 16, 128), F32),
            pltpu.VMEM((14, 256, 1024), F32),
            pltpu.VMEM((7, 8, 16, 128), F32),
            pltpu.VMEM((256, 1024), F32),
        ],
        compiler_params=pltpu.CompilerParams(vmem_limit_bytes=48 * 2**20),
    )(grad, acts, ang)


def return_kernel(
    grad, parts, out, angle_out, by_width, summed, by_tokens,
    a_send, a_recv, b_send, b_recv, c_send, c_recv,
):
    d, k, x, y, z, c = place()
    slot = c * 8 + z
    barrier = pltpu.get_barrier_semaphore()

    @pl.loop(1, 16)
    def _(i):
        pl.semaphore_signal(barrier, inc=1, device_id=(d, (k + i) % 16), device_id_type=MESH)
        pl.semaphore_signal(barrier, inc=1, device_id=((d + i) % 16, k), device_id_type=MESH)

    pl.semaphore_wait(barrier, 30)

    @pl.loop(1, 16)
    def _(i):
        to = (k + i) % 16
        to_slot = (to % 2) * 8 + to // 2
        remote(parts.at[to_slot], by_width.at[slot], b_send, b_recv, (d, to)).start()

    own_rows = pl.ds(pl.multiple_of(slot * 16, 16), 16)
    own_tokens = pl.ds(pl.multiple_of(k * 16, 16), 16)

    @pl.loop(1, 16)
    def _(i):
        to = (k + i) % 16
        to_slot = (to % 2) * 8 + to // 2
        rows = pl.ds(pl.multiple_of(to_slot * 16, 16), 16)
        remote(grad.at[rows, :], out.at[own_tokens, :], a_send, a_recv, (d, to)).start()

    out[own_tokens, :] = grad[own_rows, :]
    by_width[slot] = parts[slot]
    remote(by_width.at[0:15], by_width.at[0:15], b_send, b_recv, (d, (k + 1) % 16)).wait_recv()
    total = by_width[0]
    for i in range(1, 16):
        total = total + by_width[i]
    summed[...] = total
    by_tokens[d] = total

    @pl.loop(1, 16)
    def _(i):
        remote(summed, by_tokens.at[d], c_send, c_recv, ((d + i) % 16, k)).start()

    remote(by_tokens.at[0:15], by_tokens.at[0:15], c_send, c_recv, ((d + 1) % 16, k)).wait()
    total = by_tokens[0, 0:14, :]
    for i in range(1, 16):
        total = total + by_tokens[i, 0:14, :]
    angle_out[...] = total
    remote(by_width.at[0:15], by_width.at[0:15], b_send, b_recv, (d, (k + 1) % 16)).wait_send()
    remote(grad.at[0:240], out.at[0:240], a_send, a_recv, (d, (k + 1) % 16)).wait()


def give_back(grad, parts):
    dma = pltpu.SemaphoreType.DMA
    return pl.pallas_call(
        return_kernel,
        out_shape=(
            jax.ShapeDtypeStruct((256, 1024), BF16),
            jax.ShapeDtypeStruct((14, 512), F32),
        ),
        in_specs=[VMEM] * 2,
        out_specs=(VMEM,) * 2,
        scratch_shapes=[
            pltpu.VMEM((16, 16, 512), F32),
            pltpu.VMEM((16, 512), F32),
            pltpu.VMEM((16, 16, 512), F32),
            dma, dma, dma, dma, dma, dma,
        ],
        compiler_params=pltpu.CompilerParams(
            collective_id=1, has_side_effects=True, vmem_limit_bytes=32 * 2**20
        ),
    )(grad, parts)


def body(activations, angles, clip_bits, codes, exponents, cotangent):
    grad, acts, ang = project(
        activations, clip_bits, codes, exponents[None, :], cotangent, angles
    )
    grad, parts = butterfly(grad, acts, ang)
    return give_back(grad, parts)


def solution(mesh):
    placed = (
        P("dp", "tensor"),
        P(None, "tensor"),
        P("dp", "tensor"),
        P("tensor", "dp"),
        P(),
        P("dp", "tensor"),
    )
    return jax.shard_map(
        body,
        mesh=mesh,
        in_specs=placed,
        out_specs=(P("dp", "tensor"), P(None, "tensor")),
        check_vma=False,
    )
```

```python
import jax
import jax.numpy as jnp
from jax import lax
from jax.experimental import pallas as pl
from jax.experimental.pallas import tpu as pltpu
from jax.sharding import PartitionSpec as P

MESH = pl.DeviceIdType.MESH
F32 = jnp.float32
BF16 = jnp.bfloat16
CHUNK = 256
CHUNKS = 4


def place():
    d = lax.axis_index("dp")
    k = lax.axis_index("tensor")
    return d, k, d // 4, d % 4, k // 2, k % 2


def remote(src, dst, send, recv, to):
    return pltpu.make_async_remote_copy(
        src_ref=src, dst_ref=dst, send_sem=send, recv_sem=recv, device_id=to, device_id_type=MESH
    )


def sine_cosine(theta):
    h = theta * 0.5
    u = h * h
    s = 1.0 / 6227020800.0
    for term in (-1.0 / 39916800.0, 1.0 / 362880.0, -1.0 / 5040.0, 1.0 / 120.0, -1.0 / 6.0, 1.0):
        s = s * u + term
    s = s * h
    c = -1.0 / 87178291200.0
    for term in (1.0 / 479001600.0, -1.0 / 3628800.0, 1.0 / 40320.0, -1.0 / 720.0, 1.0 / 24.0, -0.5, 1.0):
        c = c * u + term
    return 2.0 * s * c, 1.0 - 2.0 * s * s


def squeezed(index, section):
    low = (1 << section) - 1
    return jnp.left_shift(jnp.right_shift(index, section + 1), section) | (index & low)


def lane_partner(value, section):
    lanes = lax.broadcasted_iota(jnp.int32, value.shape, 1)
    return jnp.take_along_axis(value, lanes ^ (1 << section), axis=1, mode="promise_in_bounds")


def pair_bit(section):
    return 8 if section == 10 else 1 << (section - 11)


def pairs_of(section):
    bit = pair_bit(section)
    pairs = []
    for m in range(8):
        b = section - 10
        lower = ((m >> b) << (b + 1)) | (m & ((1 << b) - 1))
        s0 = (lower % 2) * 8 + lower // 2
        pairs.append((m, s0, s0 + bit))
    return pairs


def all_kernel(
    acts, clip, codes, exps, cot, angles,
    out, angle_out,
    clip_v, exps_v, cot_v, ang_v, w_own,
    scaled, cots, w_left, w_right, w_far, sent, got, whole,
    q_in, a_in, ang, cos_t, sin_t, states, terms, tops, tall, q_back,
    parts, by_tokens, row_out, by_width, final,
    l_sem, x_send, wl_sem, wr_sem, wf_sem, b_send, b_recv, z_send, up_sem, down_sem, sib_sem,
    d_send, d_recv, e_send, e_recv, f_send, f_recv, g_send, g_recv, h_send, h_recv,
    o_send, o_recv, p_send, p_recv, r_send, r_recv, t_send, t_recv,
):
    d, k, x, y, z, c = place()
    slot = c * 8 + z
    mine16 = pl.ds(pl.multiple_of(slot * 16, 16), 16)
    own16 = pl.ds(pl.multiple_of(k * 16, 16), 16)

    def dev(px, py, pz, pc):
        return (px * 4 + py, pz * 2 + pc)

    right = dev((x + 1) % 4, y, z, c)
    left = dev((x + 3) % 4, y, z, c)
    up = dev(x, y, (z + 1) % 8, c)
    down = dev(x, y, (z + 7) % 8, c)
    sibling = dev(x, y, z, 1 - c)

    loads = [
        pltpu.make_async_copy(cot, cot_v, l_sem.at[0]),
        pltpu.make_async_copy(exps.at[:, pl.ds(pl.multiple_of(k * 640, 128), 640)], exps_v, l_sem.at[1]),
        pltpu.make_async_copy(angles, ang_v, l_sem.at[2]),
        pltpu.make_async_copy(codes, w_own, l_sem.at[3]),
        pltpu.make_async_copy(clip, clip_v, l_sem.at[4]),
    ]
    own_copy = pltpu.make_async_copy(acts.at[own16, :], a_in.at[mine16, :], l_sem.at[5])
    barrier = pltpu.get_barrier_semaphore()

    def greet(to):
        pl.semaphore_signal(barrier, inc=1, device_id=to, device_id_type=MESH)

    for copy in loads:
        copy.start()
    own_copy.start()

    @pl.loop(1, 16)
    def _(i):
        greet((d, (k + i) % 16))
        greet(((d + i) % 16, k))

    for step in range(1, 4):
        greet(dev(x, (y + step) % 4, z, 1 - c))
    pl.semaphore_wait(barrier, 33)

    def send_activations():
        @pl.loop(1, 16)
        def _(i):
            to = (k + i) % 16
            remote(
                acts.at[pl.ds(pl.multiple_of(to * 16, 16), 16), :], a_in.at[mine16, :], f_send, f_recv, (d, to)
            ).start()

    for f in range(CHUNKS):
        rows = pl.ds(f * CHUNK, CHUNK)
        remote(codes.at[rows], w_left.at[rows], x_send.at[0], wl_sem.at[f], right).start()
        remote(codes.at[rows], w_right.at[rows], x_send.at[1], wr_sem.at[f], left).start()

    for n in range(3):
        loads[n].wait()
    minus = -exps_v[...]
    scale = jnp.ones((1, 640), F32)
    for bit in range(5):
        on = jnp.bitwise_and(jnp.right_shift(minus, bit), 1) == 1
        scale = jnp.where(on, scale * (2.0 ** -(2**bit)), scale)
    scaled[...] = (cot_v[...].astype(F32) * scale).astype(BF16)

    def piece(part, token_group, half):
        start = pl.multiple_of(token_group * 256 + half * 128, 128)
        return cots.at[part, pl.ds(start, 128), :]

    owner_y = k % 4
    for half in range(2):
        mine = jnp.logical_and(owner_y == y, c == half)

        @pl.when(mine)
        def _():
            start = pl.multiple_of(y * 256 + half * 128, 128)
            cots[z // 2, pl.ds(start, 128), :] = scaled[half * 128 : (half + 1) * 128, :]

        @pl.when(jnp.logical_not(mine))
        def _():
            remote(
                scaled.at[pl.ds(half * 128, 128), :],
                piece(z // 2, y, half),
                b_send.at[half],
                b_recv.at[y],
                dev(x, owner_y, z, half),
            ).start()

    ang[c, z, 0:14, :] = ang_v[...]
    ang[c, z, 14:16, :] = jnp.zeros((2, 512), F32)

    @pl.loop(1, 8)
    def _(i):
        remote(
            ang.at[c, z], ang.at[c, z], g_send, g_recv, (d, ((z + i) % 8) * 2 + c)
        ).start()

    def to_sibling(ref):
        remote(ref, ref, z_send.at[2], sib_sem, sibling).start()

    is_source = (z % 2) == (y // 2)

    @pl.when(is_source)
    def _():
        for g in range(4):
            ref = piece(z // 2, g, c)

            @pl.when(jnp.logical_not(jnp.logical_and(y == g, y % 2 == c)))
            def _():
                remote(ref, ref, b_send.at[0], b_recv.at[g], sibling).wait_recv()

            remote(ref, ref, z_send.at[0], up_sem.at[0, g], up).start()
            remote(ref, ref, z_send.at[1], down_sem.at[0, g], down).start()
            to_sibling(ref)

    def pass_on(t):
        below = (z + 8 - t) % 8
        above = (z + t) % 8

        @pl.when((below % 2) == (y // 2))
        def _():
            for g in range(4):
                if t < 4 or g < 2:
                    ref = piece(below // 2, g, c)
                    remote(ref, ref, z_send.at[0], up_sem.at[t - 1, g], up).wait_recv()
                    if t < 3 or (t == 3 and g < 2):
                        remote(ref, ref, z_send.at[0], up_sem.at[t, g], up).start()
                    to_sibling(ref)
                if t < 4 or g >= 2:
                    ref = piece(above // 2, g, c)
                    remote(ref, ref, z_send.at[1], down_sem.at[t - 1, g], down).wait_recv()
                    if t < 3 or (t == 3 and g >= 2):
                        remote(ref, ref, z_send.at[1], down_sem.at[t, g], down).start()
                    to_sibling(ref)

    def forward(f):
        rows = pl.ds(f * CHUNK, CHUNK)
        if f % 2 == 0:
            remote(w_left.at[rows], w_left.at[rows], x_send.at[0], wl_sem.at[f], right).wait_recv()
            remote(w_left.at[rows], w_far.at[rows], x_send.at[2], wf_sem.at[f], right).start()
        else:
            remote(w_right.at[rows], w_right.at[rows], x_send.at[1], wr_sem.at[f], left).wait_recv()
            remote(w_right.at[rows], w_far.at[rows], x_send.at[3], wf_sem.at[f], left).start()

    pass_on(1)
    pass_on(2)
    forward(0)
    forward(1)
    pass_on(3)
    send_activations()

    remote(ang.at[0, 0:7], ang.at[0, 0:7], g_send, g_recv, sibling).wait_recv()
    remote(ang.at[c], ang.at[c], h_send, h_recv, sibling).start()
    forward(2)
    forward(3)
    pass_on(4)
    remote(ang.at[0], ang.at[0], h_send, h_recv, sibling).wait_recv()
    lane_row = lax.broadcasted_iota(jnp.int32, (128, 128), 1)
    lane_col = lax.broadcasted_iota(jnp.int32, (128, 128), 0)
    for s in range(7):
        rows = jnp.concatenate(
            [ang[core, :, s, a * 128 : (a + 1) * 128] for a in range(4) for core in range(2)], axis=0
        )
        for b in range(2):
            pick = jnp.where(lane_col == b * 64 + squeezed(lane_row, s), 1.0, 0.0)
            theta = jnp.dot(rows, pick, precision=lax.Precision.HIGHEST, preferred_element_type=F32)
            sine, cosine = sine_cosine(theta)
            upper = (lax.broadcasted_iota(jnp.int32, theta.shape, 1) & (1 << s)) != 0
            signed = jnp.where(upper, sine, -sine)
            for a in range(4):
                cos_t[s, 2 * a + b] = cosine[a * 16 : (a + 1) * 16]
                sin_t[s, 2 * a + b] = signed[a * 16 : (a + 1) * 16]
    for s in range(7, 14):
        for a in range(4):
            for core in range(2):
                sine, cosine = sine_cosine(ang[core, :, s, a * 128 : (a + 1) * 128])
                cos_t[s, a, core * 8 : core * 8 + 8] = cosine
                sin_t[s, a, core * 8 : core * 8 + 8] = sine


    remote(cots.at[0:2], cots.at[0:2], z_send.at[2], sib_sem, sibling).wait_recv()

    def finish(f):
        lanes = pl.ds(pl.multiple_of(f * CHUNK, CHUNK), CHUNK)
        remote(got.at[f], got.at[f], d_send, d_recv.at[f], sibling).wait_recv()
        place_in_word = lax.broadcasted_iota(jnp.int32, (16, CHUNK), 0)

        def masked(w):
            rows = pl.ds(pl.multiple_of(w * 16, 16), 16)
            total = whole[f, rows, :]
            for j in range(3):
                total = total + got[f, j, rows, :].astype(F32)
            word = jnp.broadcast_to(clip_v[pl.ds(w, 1), lanes], (16, CHUNK))
            bit = jnp.bitwise_and(jnp.right_shift(word, place_in_word), 1)
            return rows, jnp.where(bit == 1, total, 0.0)

        @pl.loop(1, 16)
        def _(i):
            to = (k + i) % 16
            rows, value = masked(to)
            whole[f, rows, :] = value
            remote(
                whole.at[f, rows, :], q_in.at[mine16, lanes], e_send, e_recv, (d, to)
            ).start()

        _, value = masked(k)
        q_in[mine16, lanes] = value

    loads[3].wait()
    loads[4].wait()
    own_copy.wait()

    @pl.loop(0, 4 * CHUNKS)
    def _(i):
        f = i // 4
        j = i % 4
        to_y = (y + j + 1) % 4
        rows = pl.ds(pl.multiple_of(f * CHUNK, CHUNK), CHUNK)
        tokens = pl.ds(pl.multiple_of(to_y * 256, 256), 256)

        @pl.when(j == 0)
        def _():
            @pl.when(f % 2 == 1)
            def _():
                remote(w_left.at[rows], w_left.at[rows], x_send.at[0], wl_sem.at[f], right).wait_recv()

            @pl.when(f % 2 == 0)
            def _():
                remote(w_right.at[rows], w_right.at[rows], x_send.at[1], wr_sem.at[f], left).wait_recv()

            remote(w_far.at[rows], w_far.at[rows], x_send.at[2], wf_sem.at[f], right).wait_recv()

        def product(part, ref):
            return lax.dot_general(
                cots[part, tokens, :], ref[rows, :], (((1,), (1,)), ((), ())),
                preferred_element_type=F32,
            )

        total = product(x, w_own)
        total = total + product((x + 3) % 4, w_left)
        total = total + product((x + 1) % 4, w_right)
        total = total + product((x + 2) % 4, w_far)

        @pl.when(j < 3)
        def _():
            sent[f, j] = total.astype(BF16)
            remote(
                sent.at[f, j], got.at[f, j], d_send, d_recv.at[f], dev(x, to_y, z, c)
            ).start()

        @pl.when(j == 3)
        def _():
            whole[f] = total

            @pl.when(f > 0)
            def _():
                finish(f - 1)

    finish(CHUNKS - 1)

    remote(a_in.at[0:240], a_in.at[0:240], f_send, f_recv, sibling).wait()

    def row(table, s, tile, index):
        return jnp.broadcast_to(table[s, tile, pl.ds(index, 1), :], (16, 128))

    @pl.loop(0, 16)
    def _(kk):
        rows = pl.ds(pl.multiple_of(kk * 16, 16), 16)
        field = [a_in[rows, t * 128 : (t + 1) * 128].astype(F32) for t in range(8)]
        for s in range(7):
            for t in range(8):
                field[t] = row(cos_t, s, t, kk) * field[t] + row(sin_t, s, t, kk) * lane_partner(field[t], s)
                states[s, rows, t * 128 : (t + 1) * 128] = field[t]
        for s in range(7, 10):
            b = s - 7
            for a in range(4):
                lo = ((a >> b) << (b + 1)) | (a & ((1 << b) - 1))
                hi = lo + (1 << b)
                cosine, sine = row(cos_t, s, a, kk), row(sin_t, s, a, kk)
                field[lo], field[hi] = (
                    cosine * field[lo] - sine * field[hi],
                    sine * field[lo] + cosine * field[hi],
                )
            for t in range(8):
                states[s, rows, t * 128 : (t + 1) * 128] = field[t]

    def fixed_row(table, s, t, m):
        return jnp.broadcast_to(table[s, t % 4, pl.ds((t // 4) * 8 + m, 1), :], (8, 128))

    def halves(lo, hi):
        for half in range(2):
            yield slice(lo * 16 + half * 8, lo * 16 + half * 8 + 8), slice(hi * 16 + half * 8, hi * 16 + half * 8 + 8)

    @pl.loop(0, 8)
    def _(t):
        lanes = pl.ds(pl.multiple_of(t * 128, 128), 128)
        for s in range(10, 14):
            for m, lo, hi in pairs_of(s):
                cosine, sine = fixed_row(cos_t, s, t, m), fixed_row(sin_t, s, t, m)
                for lo_rows, hi_rows in halves(lo, hi):
                    v_lo, v_hi = states[s - 1, lo_rows, lanes], states[s - 1, hi_rows, lanes]
                    states[s, lo_rows, lanes] = cosine * v_lo - sine * v_hi
                    states[s, hi_rows, lanes] = sine * v_lo + cosine * v_hi

    remote(q_in.at[0:240], q_in.at[0:240], e_send, e_recv, sibling).wait()

    def to_section_owner(s):
        @pl.when(d != s)
        def _():
            remote(parts.at[s], by_tokens.at[d], p_send, p_recv, (s, k)).start()

        @pl.when(d == s)
        def _():
            by_tokens[d] = parts[s]

    @pl.loop(0, 8)
    def _(t):
        lanes = pl.ds(pl.multiple_of(t * 128, 128), 128)
        for s in (13, 12, 11, 10):
            source = q_in if s == 13 else tall
            for m, lo, hi in pairs_of(s):
                cosine, sine = fixed_row(cos_t, s, t, m), fixed_row(sin_t, s, t, m)
                total = None
                for lo_rows, hi_rows in halves(lo, hi):
                    q_lo, q_hi = source[lo_rows, lanes], source[hi_rows, lanes]
                    term = q_hi * states[s, lo_rows, lanes] - q_lo * states[s, hi_rows, lanes]
                    total = term if total is None else total + term
                    tall[lo_rows, lanes] = cosine * q_lo + sine * q_hi
                    tall[hi_rows, lanes] = cosine * q_hi - sine * q_lo
                tops[s - 7, t % 4, pl.ds((t // 4) * 8 + m, 1), :] = jnp.sum(total, axis=0, keepdims=True)

    def laid_out(first, last):
        for s in range(first, last):
            for a in range(4):
                parts[s, :, a * 128 : (a + 1) * 128] = tops[s - 7, a]

    laid_out(10, 14)

    @pl.loop(0, 4)
    def _(i):
        to_section_owner(10 + (d + i) % 4)

    @pl.loop(0, 16)
    def _(i):
        kk = (slot + 1 + i) % 16
        rows = pl.ds(pl.multiple_of(kk * 16, 16), 16)
        grad = [tall[rows, t * 128 : (t + 1) * 128] for t in range(8)]
        for s in (9, 8, 7):
            b = s - 7
            for a in range(4):
                lo = ((a >> b) << (b + 1)) | (a & ((1 << b) - 1))
                hi = lo + (1 << b)
                cosine, sine = row(cos_t, s, a, kk), row(sin_t, s, a, kk)
                term = grad[hi] * states[s, rows, lo * 128 : (lo + 1) * 128]
                term = term - grad[lo] * states[s, rows, hi * 128 : (hi + 1) * 128]
                tops[s - 7, a, pl.ds(kk, 1), :] = jnp.sum(term, axis=0, keepdims=True)
                grad[lo], grad[hi] = (
                    cosine * grad[lo] + sine * grad[hi],
                    cosine * grad[hi] - sine * grad[lo],
                )
        for s in (6, 5, 4, 3, 2, 1, 0):
            for t in range(8):
                other = lane_partner(grad[t], s)
                term = other * states[s, rows, t * 128 : (t + 1) * 128]
                terms[s, t, pl.ds(kk, 1), :] = jnp.sum(term, axis=0, keepdims=True)
                grad[t] = row(cos_t, s, t, kk) * grad[t] - row(sin_t, s, t, kk) * other
        for t in range(8):
            q_back[rows, t * 128 : (t + 1) * 128] = grad[t].astype(BF16)

        @pl.when(i < 15)
        def _():
            to = (kk % 8) * 2 + kk // 8
            remote(q_back.at[rows, :], out.at[own16, :], o_send, o_recv, (d, to)).start()

        @pl.when(i == 15)
        def _():
            out[own16, :] = q_back[rows, :]

    laid_out(7, 10)
    for s in range(7):
        sign = jnp.where((lane_col & (1 << s)) == 0, 1.0, -1.0)
        total = None
        for b in range(2):
            pick = jnp.where(lane_row == b * 64 + squeezed(lane_col, s), sign, 0.0)
            rows = jnp.concatenate([terms[s, 2 * a + b] for a in range(4)], axis=0)
            part = jnp.dot(rows, pick, precision=lax.Precision.HIGHEST, preferred_element_type=F32)
            total = part if total is None else total + part
        for a in range(4):
            parts[s, :, a * 128 : (a + 1) * 128] = total[a * 16 : (a + 1) * 16]

    @pl.loop(0, 10)
    def _(i):
        to_section_owner((d + i) % 10)

    @pl.when(d < 14)
    def _():
        remote(by_tokens.at[0:15], by_tokens.at[0:15], p_send, p_recv, sibling).wait_recv()
        total = by_tokens[0]
        for i in range(1, 16):
            total = total + by_tokens[i]
        for j in range(16):
            row_out[j] = total[j : j + 1, :]

        @pl.loop(1, 16)
        def _(i):
            other = (slot + i) % 16
            remote(
                row_out.at[other], by_width.at[slot], r_send, r_recv, (d, (other % 8) * 2 + other // 8)
            ).start()

        by_width[slot] = row_out[slot]
        remote(by_width.at[0:15], by_width.at[0:15], r_send, r_recv, sibling).wait_recv()
        total = by_width[0]
        for i in range(1, 16):
            total = total + by_width[i]
        final[d] = total

        @pl.loop(1, 16)
        def _(i):
            remote(final.at[d], final.at[d], t_send, t_recv, ((d + i) % 16, k)).start()

        remote(final.at[0:13], final.at[0:13], t_send, t_recv, sibling).wait_recv()
        remote(by_tokens.at[0:13], by_tokens.at[0:13], p_send, p_recv, sibling).wait_send()
        remote(by_width.at[0:15], by_width.at[0:15], r_send, r_recv, sibling).wait_send()
        remote(final.at[0:15], final.at[0:15], t_send, t_recv, sibling).wait_send()

    @pl.when(d >= 14)
    def _():
        remote(final.at[0:14], final.at[0:14], t_send, t_recv, sibling).wait_recv()
        remote(by_tokens.at[0:14], by_tokens.at[0:14], p_send, p_recv, sibling).wait_send()

    for s in range(14):
        angle_out[s : s + 1, :] = final[s]

    remote(q_back.at[0:240], out.at[0:240], o_send, o_recv, sibling).wait()
    remote(ang.at[0, 0:7], ang.at[0, 0:7], g_send, g_recv, sibling).wait_send()
    remote(ang.at[0], ang.at[0], h_send, h_recv, sibling).wait_send()
    remote(sent, got, d_send, d_recv.at[0], sibling).wait_send()
    remote(w_own, w_left, x_send.at[0], wl_sem.at[0], right).wait_send()
    remote(w_own, w_right, x_send.at[1], wr_sem.at[0], left).wait_send()
    half_rows = pl.ds(0, 512)
    remote(w_left.at[half_rows], w_far.at[half_rows], x_send.at[2], wf_sem.at[0], right).wait_send()
    remote(w_left.at[half_rows], w_far.at[half_rows], x_send.at[3], wf_sem.at[0], left).wait_send()
    for half in range(2):
        @pl.when(jnp.logical_not(jnp.logical_and(owner_y == y, c == half)))
        def _():
            ref = scaled.at[pl.ds(half * 128, 128), :]
            remote(ref, ref, b_send.at[half], b_recv.at[0], sibling).wait_send()
    for way in range(2):
        @pl.when(is_source)
        def _():
            remote(cots.at[0], cots.at[0], z_send.at[way], sib_sem, sibling).wait_send()

        @pl.when(jnp.logical_not(is_source))
        def _():
            ref = cots.at[0, 0:768, :]
            remote(ref, ref, z_send.at[way], sib_sem, sibling).wait_send()
    remote(cots.at[0:2], cots.at[0:2], z_send.at[2], sib_sem, sibling).wait_send()


VMEM = pl.BlockSpec(memory_space=pltpu.VMEM)
HBM = pl.BlockSpec(memory_space=pltpu.HBM)


def body(activations, angles, clip_bits, codes, exponents, cotangent):
    dma = pltpu.SemaphoreType.DMA
    return pl.pallas_call(
        all_kernel,
        out_shape=(
            jax.ShapeDtypeStruct((256, 1024), BF16),
            jax.ShapeDtypeStruct((14, 512), F32),
        ),
        in_specs=[HBM] * 6,
        out_specs=(VMEM,) * 2,
        scratch_shapes=[
            pltpu.VMEM((16, 1024), jnp.int32),
            pltpu.VMEM((1, 640), jnp.int32),
            pltpu.VMEM((256, 640), BF16),
            pltpu.VMEM((14, 512), F32),
            pltpu.VMEM((1024, 640), BF16),
            pltpu.VMEM((256, 640), BF16),
            pltpu.VMEM((4, 1024, 640), BF16),
            pltpu.VMEM((1024, 640), BF16),
            pltpu.VMEM((1024, 640), BF16),
            pltpu.VMEM((1024, 640), BF16),
            pltpu.VMEM((CHUNKS, 3, 256, CHUNK), BF16),
            pltpu.VMEM((CHUNKS, 3, 256, CHUNK), BF16),
            pltpu.VMEM((CHUNKS, 256, CHUNK), F32),
            pltpu.VMEM((256, 1024), F32),
            pltpu.VMEM((256, 1024), BF16),
            pltpu.VMEM((2, 8, 16, 512), F32),
            pltpu.VMEM((14, 8, 16, 128), F32),
            pltpu.VMEM((14, 8, 16, 128), F32),
            pltpu.VMEM((14, 256, 1024), F32),
            pltpu.VMEM((7, 8, 16, 128), F32),
            pltpu.VMEM((7, 4, 16, 128), F32),
            pltpu.VMEM((256, 1024), F32),
            pltpu.VMEM((256, 1024), BF16),
            pltpu.VMEM((14, 16, 512), F32),
            pltpu.VMEM((16, 16, 512), F32),
            pltpu.VMEM((16, 1, 512), F32),
            pltpu.VMEM((16, 1, 512), F32),
            pltpu.VMEM((16, 1, 512), F32),
            dma((6,)), dma((4,)), dma((CHUNKS,)), dma((CHUNKS,)), dma((CHUNKS,)),
            dma((2,)), dma((4,)), dma((3,)), dma((4, 4)), dma((4, 4)), dma,
            dma, dma((CHUNKS,)), dma, dma, dma, dma, dma, dma, dma, dma,
            dma, dma, dma, dma, dma, dma, dma, dma,
        ],
        compiler_params=pltpu.CompilerParams(
            collective_id=0, has_side_effects=True, vmem_limit_bytes=56 * 2**20
        ),
        cost_estimate=pl.CostEstimate(flops=5400000000, bytes_accessed=6000000, transcendentals=0),
    )(activations, clip_bits, codes, exponents[None, :], cotangent, angles)


def solution(mesh):
    placed = (
        P("dp", "tensor"),
        P(None, "tensor"),
        P("dp", "tensor"),
        P("tensor", "dp"),
        P(),
        P("dp", "tensor"),
    )
    return jax.shard_map(
        body,
        mesh=mesh,
        in_specs=placed,
        out_specs=(P("dp", "tensor"), P(None, "tensor")),
        check_vma=False,
    )
```

```python
import jax
import jax.numpy as jnp
from jax import lax
from jax.experimental import pallas as pl
from jax.experimental.pallas import tpu as pltpu
from jax.sharding import PartitionSpec as P

MESH = pl.DeviceIdType.MESH
F32 = jnp.float32
BF16 = jnp.bfloat16
CHUNK = 256
CHUNKS = 4
ORDER = (2, 1, 3, 0)


def place():
    d = lax.axis_index("dp")
    k = lax.axis_index("tensor")
    return d, k, d // 4, d % 4, k // 2, k % 2


def remote(src, dst, send, recv, to):
    return pltpu.make_async_remote_copy(
        src_ref=src, dst_ref=dst, send_sem=send, recv_sem=recv, device_id=to, device_id_type=MESH
    )


def sine_cosine(theta):
    h = theta * 0.5
    u = h * h
    s = 1.0 / 6227020800.0
    for term in (-1.0 / 39916800.0, 1.0 / 362880.0, -1.0 / 5040.0, 1.0 / 120.0, -1.0 / 6.0, 1.0):
        s = s * u + term
    s = s * h
    c = -1.0 / 87178291200.0
    for term in (1.0 / 479001600.0, -1.0 / 3628800.0, 1.0 / 40320.0, -1.0 / 720.0, 1.0 / 24.0, -0.5, 1.0):
        c = c * u + term
    return 2.0 * s * c, 1.0 - 2.0 * s * s


def squeezed(index, section):
    low = (1 << section) - 1
    return jnp.left_shift(jnp.right_shift(index, section + 1), section) | (index & low)


def lane_partner(value, section):
    lanes = lax.broadcasted_iota(jnp.int32, value.shape, 1)
    return jnp.take_along_axis(value, lanes ^ (1 << section), axis=1, mode="promise_in_bounds")


def pair_bit(section):
    return 8 if section == 10 else 1 << (section - 11)


def pairs_of(section):
    bit = pair_bit(section)
    pairs = []
    for m in range(8):
        b = section - 10
        lower = ((m >> b) << (b + 1)) | (m & ((1 << b) - 1))
        s0 = (lower % 2) * 8 + lower // 2
        pairs.append((m, s0, s0 + bit))
    return pairs


def all_kernel(
    acts, clip, codes, exps, cot, angles,
    out, angle_out,
    clip_v, exps_v, cot_v, ang_v, w_own,
    scaled, cots, w_left, w_right, w_far, sent, got, steps, got_steps, whole, narrow,
    q_in, a_in, ang, cos_t, sin_t, states, terms, tops, tall, q_back,
    parts, by_tokens, row_out, by_width, final,
    l_sem, x_send, wl_sem, wr_sem, wf_sem, b_send, b_recv, z_send, up_sem, down_sem, sib_sem,
    s_send, s_recv, d_send, d_recv, e_send, e_recv, f_send, f_recv, g_send, g_recv, h_send, h_recv,
    o_send, o_recv, p_send, p_recv, r_send, r_recv, t_send, t_recv,
):
    d, k, x, y, z, c = place()
    slot = c * 8 + z
    mine16 = pl.ds(pl.multiple_of(slot * 16, 16), 16)
    own16 = pl.ds(pl.multiple_of(k * 16, 16), 16)

    def dev(px, py, pz, pc):
        return (px * 4 + py, pz * 2 + pc)

    right = dev((x + 1) % 4, y, z, c)
    left = dev((x + 3) % 4, y, z, c)
    up = dev(x, y, (z + 1) % 8, c)
    down = dev(x, y, (z + 7) % 8, c)
    sibling = dev(x, y, z, 1 - c)

    loads = [
        pltpu.make_async_copy(cot, cot_v, l_sem.at[0]),
        pltpu.make_async_copy(exps.at[:, pl.ds(pl.multiple_of(k * 640, 128), 640)], exps_v, l_sem.at[1]),
        pltpu.make_async_copy(angles, ang_v, l_sem.at[2]),
        pltpu.make_async_copy(codes, w_own, l_sem.at[3]),
        pltpu.make_async_copy(clip, clip_v, l_sem.at[4]),
    ]
    own_copy = pltpu.make_async_copy(acts.at[own16, :], a_in.at[mine16, :], l_sem.at[5])
    barrier = pltpu.get_barrier_semaphore()

    def greet(to):
        pl.semaphore_signal(barrier, inc=1, device_id=to, device_id_type=MESH)

    for copy in loads:
        copy.start()
    own_copy.start()

    @pl.loop(1, 16)
    def _(i):
        greet((d, (k + i) % 16))
        greet(((d + i) % 16, k))

    for step in range(1, 4):
        greet(dev(x, (y + step) % 4, z, 1 - c))
    pl.semaphore_wait(barrier, 33)

    def send_activations():
        @pl.loop(1, 16)
        def _(i):
            to = (k + i) % 16
            remote(
                acts.at[pl.ds(pl.multiple_of(to * 16, 16), 16), :], a_in.at[mine16, :], f_send, f_recv, (d, to)
            ).start()

    for f in range(CHUNKS):
        rows = pl.ds(f * CHUNK, CHUNK)
        remote(codes.at[rows], w_left.at[rows], x_send.at[0], wl_sem.at[f], right).start()
        remote(codes.at[rows], w_right.at[rows], x_send.at[1], wr_sem.at[f], left).start()

    for n in range(3):
        loads[n].wait()
    minus = -exps_v[...]
    scale = jnp.ones((1, 640), F32)
    for bit in range(5):
        on = jnp.bitwise_and(jnp.right_shift(minus, bit), 1) == 1
        scale = jnp.where(on, scale * (2.0 ** -(2**bit)), scale)
    scaled[...] = (cot_v[...].astype(F32) * scale).astype(BF16)

    def piece(part, token_group, half):
        start = pl.multiple_of(token_group * 256 + half * 128, 128)
        return cots.at[part, pl.ds(start, 128), :]

    owner_y = k % 4
    for half in range(2):
        mine = jnp.logical_and(owner_y == y, c == half)

        @pl.when(mine)
        def _():
            start = pl.multiple_of(y * 256 + half * 128, 128)
            cots[z // 2, pl.ds(start, 128), :] = scaled[half * 128 : (half + 1) * 128, :]

        @pl.when(jnp.logical_not(mine))
        def _():
            remote(
                scaled.at[pl.ds(half * 128, 128), :],
                piece(z // 2, y, half),
                b_send.at[half],
                b_recv.at[y],
                dev(x, owner_y, z, half),
            ).start()

    ang[c, z, 0:14, :] = ang_v[...]
    ang[c, z, 14:16, :] = jnp.zeros((2, 512), F32)

    @pl.loop(1, 8)
    def _(i):
        remote(
            ang.at[c, z], ang.at[c, z], g_send, g_recv, (d, ((z + i) % 8) * 2 + c)
        ).start()

    def to_sibling(ref, n):
        remote(ref, ref, z_send.at[2], sib_sem.at[n], sibling).start()

    is_source = (z % 2) == (y // 2)

    def group(n):
        return (y + ORDER[n]) % 4

    @pl.when(is_source)
    def _():
        for n in range(4):
            g = group(n)
            ref = piece(z // 2, g, c)

            @pl.when(jnp.logical_not(jnp.logical_and(y == g, y % 2 == c)))
            def _():
                remote(ref, ref, b_send.at[0], b_recv.at[g], sibling).wait_recv()

            remote(ref, ref, z_send.at[0], up_sem.at[0, n], up).start()
            remote(ref, ref, z_send.at[1], down_sem.at[0, n], down).start()
            to_sibling(ref, n)

    def pass_on(t, n):
        below = (z + 8 - t) % 8
        above = (z + t) % 8

        @pl.when((below % 2) == (y // 2))
        def _():
            if t < 4 or n % 2 == 0:
                ref = piece(below // 2, group(n), c)
                remote(ref, ref, z_send.at[0], up_sem.at[t - 1, n], up).wait_recv()
                if t < 3 or (t == 3 and n % 2 == 0):
                    remote(ref, ref, z_send.at[0], up_sem.at[t, n], up).start()
                to_sibling(ref, n)
            if t < 4 or n % 2 == 1:
                ref = piece(above // 2, group(n), c)
                remote(ref, ref, z_send.at[1], down_sem.at[t - 1, n], down).wait_recv()
                if t < 3 or (t == 3 and n % 2 == 1):
                    remote(ref, ref, z_send.at[1], down_sem.at[t, n], down).start()
                to_sibling(ref, n)

    def group_here(n):
        remote(cots.at[0, 0:512, :], cots.at[0, 0:512, :], z_send.at[2], sib_sem.at[n], sibling).wait_recv()

    def forward(f):
        rows = pl.ds(f * CHUNK, CHUNK)
        if f % 2 == 0:
            remote(w_left.at[rows], w_left.at[rows], x_send.at[0], wl_sem.at[f], right).wait_recv()
            remote(w_left.at[rows], w_far.at[rows], x_send.at[2], wf_sem.at[f], right).start()
        else:
            remote(w_right.at[rows], w_right.at[rows], x_send.at[1], wr_sem.at[f], left).wait_recv()
            remote(w_right.at[rows], w_far.at[rows], x_send.at[3], wf_sem.at[f], left).start()

    def chunk_here(f):
        rows = pl.ds(f * CHUNK, CHUNK)
        if f % 2 == 1:
            remote(w_left.at[rows], w_left.at[rows], x_send.at[0], wl_sem.at[f], right).wait_recv()
        else:
            remote(w_right.at[rows], w_right.at[rows], x_send.at[1], wr_sem.at[f], left).wait_recv()
        remote(w_far.at[rows], w_far.at[rows], x_send.at[2], wf_sem.at[f], right).wait_recv()

    def product(f, n):
        rows = pl.ds(pl.multiple_of(f * CHUNK, CHUNK), CHUNK)
        to_y = (y + jnp.where(n == 3, 0, jnp.where(n == 0, 2, jnp.where(n == 1, 1, 3)))) % 4
        tokens = pl.ds(pl.multiple_of(to_y * 256, 256), 256)

        def part(index, ref):
            return lax.dot_general(
                cots[index, tokens, :], ref[rows, :], (((1,), (1,)), ((), ())),
                preferred_element_type=F32,
            )

        total = part(x, w_own)
        total = total + part((x + 3) % 4, w_left)
        total = total + part((x + 1) % 4, w_right)
        return to_y, total + part((x + 2) % 4, w_far)

    def to_row(f, n):
        to_y, total = product(f, n)
        most = jnp.max(jnp.max(jnp.abs(total), axis=0, keepdims=True), axis=1, keepdims=True)
        most = jnp.maximum(most, 1e-30)
        sent[f, n] = jnp.round(total * (32000.0 / most)).astype(jnp.int32).astype(jnp.int16)
        steps[f, n] = jnp.broadcast_to(most * (1.0 / 32000.0), (1, 128))
        remote(steps.at[f, n], got_steps.at[f, n], s_send, s_recv.at[f], dev(x, to_y, z, c)).start()
        remote(sent.at[f, n], got.at[f, n], d_send, d_recv.at[f], dev(x, to_y, z, c)).start()

    lane_row = lax.broadcasted_iota(jnp.int32, (128, 128), 1)
    lane_col = lax.broadcasted_iota(jnp.int32, (128, 128), 0)

    def low_tables(first, last):
        for s in range(first, last):
            rows = jnp.concatenate(
                [ang[core, :, s, a * 128 : (a + 1) * 128] for a in range(4) for core in range(2)], axis=0
            )
            for b in range(2):
                pick = jnp.where(lane_col == b * 64 + squeezed(lane_row, s), 1.0, 0.0)
                theta = jnp.dot(rows, pick, precision=lax.Precision.HIGHEST, preferred_element_type=F32)
                sine, cosine = sine_cosine(theta)
                upper = (lax.broadcasted_iota(jnp.int32, theta.shape, 1) & (1 << s)) != 0
                signed = jnp.where(upper, sine, -sine)
                for a in range(4):
                    cos_t[s, 2 * a + b] = cosine[a * 16 : (a + 1) * 16]
                    sin_t[s, 2 * a + b] = signed[a * 16 : (a + 1) * 16]

    def high_tables():
        for s in range(7, 14):
            for a in range(4):
                for core in range(2):
                    sine, cosine = sine_cosine(ang[core, :, s, a * 128 : (a + 1) * 128])
                    cos_t[s, a, core * 8 : core * 8 + 8] = cosine
                    sin_t[s, a, core * 8 : core * 8 + 8] = sine

    pass_on(1, 0)
    pass_on(2, 0)
    pass_on(1, 1)
    forward(0)
    forward(1)
    pass_on(3, 0)
    remote(ang.at[0, 0:7], ang.at[0, 0:7], g_send, g_recv, sibling).wait_recv()
    remote(ang.at[c], ang.at[c], h_send, h_recv, sibling).start()
    pass_on(2, 1)
    pass_on(4, 0)
    pass_on(1, 2)
    remote(ang.at[0], ang.at[0], h_send, h_recv, sibling).wait_recv()
    pass_on(3, 1)
    loads[3].wait()
    loads[4].wait()
    own_copy.wait()
    group_here(0)
    chunk_here(0)
    to_row(0, 0)
    forward(2)
    pass_on(2, 2)
    chunk_here(1)
    to_row(1, 0)
    pass_on(4, 1)
    forward(3)
    pass_on(1, 3)
    low_tables(0, 2)
    pass_on(3, 2)
    group_here(1)

    @pl.loop(0, 2)
    def _(f):
        to_row(f, 1)

    pass_on(2, 3)
    low_tables(2, 4)
    pass_on(4, 2)
    pass_on(3, 3)
    send_activations()
    low_tables(4, 7)
    chunk_here(2)

    @pl.loop(0, 2)
    def _(n):
        to_row(2, n)

    group_here(2)

    @pl.loop(0, 3)
    def _(f):
        to_row(f, 2)

    pass_on(4, 3)
    high_tables()
    chunk_here(3)

    @pl.loop(0, 3)
    def _(n):
        to_row(3, n)

    group_here(3)

    def finish(f):
        lanes = pl.ds(pl.multiple_of(f * CHUNK, CHUNK), CHUNK)
        remote(steps.at[f], got_steps.at[f], s_send, s_recv.at[f], sibling).wait_recv()
        remote(got.at[f], got.at[f], d_send, d_recv.at[f], sibling).wait_recv()
        place_in_word = lax.broadcasted_iota(jnp.int32, (16, CHUNK), 0)

        def masked(w):
            rows = pl.ds(pl.multiple_of(w * 16, 16), 16)
            total = whole[f, rows, :]
            for j in range(3):
                step = jnp.concatenate([got_steps[f, j], got_steps[f, j]], axis=1)
                total = total + got[f, j, rows, :].astype(jnp.int32).astype(F32) * step
            word = jnp.broadcast_to(clip_v[pl.ds(w, 1), lanes], (16, CHUNK))
            bit = jnp.bitwise_and(jnp.right_shift(word, place_in_word), 1)
            return rows, jnp.where(bit == 1, total, 0.0)

        @pl.loop(1, 16)
        def _(i):
            to = (k + i) % 16
            rows, value = masked(to)
            narrow[f, rows, :] = value.astype(BF16)
            remote(
                narrow.at[f, rows, :], q_in.at[mine16, lanes], e_send, e_recv, (d, to)
            ).start()

        _, value = masked(k)
        q_in[mine16, lanes] = value.astype(BF16)

    @pl.loop(0, CHUNKS)
    def _(f):
        _, total = product(f, 3)
        whole[f] = total
        finish(f)

    remote(a_in.at[0:240], a_in.at[0:240], f_send, f_recv, sibling).wait()

    def row(table, s, tile, index):
        return jnp.broadcast_to(table[s, tile, pl.ds(index, 1), :], (16, 128))

    @pl.loop(0, 16)
    def _(kk):
        rows = pl.ds(pl.multiple_of(kk * 16, 16), 16)
        field = [a_in[rows, t * 128 : (t + 1) * 128].astype(F32) for t in range(8)]
        for s in range(7):
            for t in range(8):
                field[t] = row(cos_t, s, t, kk) * field[t] + row(sin_t, s, t, kk) * lane_partner(field[t], s)
                states[s, rows, t * 128 : (t + 1) * 128] = field[t]
        for s in range(7, 10):
            b = s - 7
            for a in range(4):
                lo = ((a >> b) << (b + 1)) | (a & ((1 << b) - 1))
                hi = lo + (1 << b)
                cosine, sine = row(cos_t, s, a, kk), row(sin_t, s, a, kk)
                field[lo], field[hi] = (
                    cosine * field[lo] - sine * field[hi],
                    sine * field[lo] + cosine * field[hi],
                )
            for t in range(8):
                states[s, rows, t * 128 : (t + 1) * 128] = field[t]

    def fixed_row(table, s, t, m):
        return jnp.broadcast_to(table[s, t % 4, pl.ds((t // 4) * 8 + m, 1), :], (16, 128))

    def halves(lo, hi):
        yield slice(lo * 16, lo * 16 + 16), slice(hi * 16, hi * 16 + 16)

    @pl.loop(0, 8)
    def _(t):
        lanes = pl.ds(pl.multiple_of(t * 128, 128), 128)
        for s in range(10, 14):
            for m, lo, hi in pairs_of(s):
                cosine, sine = fixed_row(cos_t, s, t, m), fixed_row(sin_t, s, t, m)
                for lo_rows, hi_rows in halves(lo, hi):
                    v_lo, v_hi = states[s - 1, lo_rows, lanes], states[s - 1, hi_rows, lanes]
                    states[s, lo_rows, lanes] = cosine * v_lo - sine * v_hi
                    states[s, hi_rows, lanes] = sine * v_lo + cosine * v_hi

    remote(q_in.at[0:240], q_in.at[0:240], e_send, e_recv, sibling).wait()

    def to_section_owner(s):
        @pl.when(d != s)
        def _():
            remote(parts.at[s], by_tokens.at[d], p_send, p_recv, (s, k)).start()

        @pl.when(d == s)
        def _():
            by_tokens[d] = parts[s]

    @pl.loop(0, 8)
    def _(t):
        lanes = pl.ds(pl.multiple_of(t * 128, 128), 128)
        for s in (13, 12, 11, 10):
            source = q_in if s == 13 else tall
            for m, lo, hi in pairs_of(s):
                cosine, sine = fixed_row(cos_t, s, t, m), fixed_row(sin_t, s, t, m)
                total = None
                for lo_rows, hi_rows in halves(lo, hi):
                    q_lo, q_hi = source[lo_rows, lanes].astype(F32), source[hi_rows, lanes].astype(F32)
                    term = q_hi * states[s, lo_rows, lanes] - q_lo * states[s, hi_rows, lanes]
                    total = term if total is None else total + term
                    tall[lo_rows, lanes] = cosine * q_lo + sine * q_hi
                    tall[hi_rows, lanes] = cosine * q_hi - sine * q_lo
                tops[s - 7, t % 4, pl.ds((t // 4) * 8 + m, 1), :] = jnp.sum(total, axis=0, keepdims=True)

    def laid_out(first, last):
        for s in range(first, last):
            for a in range(4):
                parts[s, :, a * 128 : (a + 1) * 128] = tops[s - 7, a]

    laid_out(10, 14)

    @pl.loop(0, 4)
    def _(i):
        to_section_owner(10 + (d + i) % 4)

    @pl.loop(0, 16)
    def _(i):
        kk = (slot + 1 + i) % 16
        rows = pl.ds(pl.multiple_of(kk * 16, 16), 16)
        grad = [tall[rows, t * 128 : (t + 1) * 128] for t in range(8)]
        for s in (9, 8, 7):
            b = s - 7
            for a in range(4):
                lo = ((a >> b) << (b + 1)) | (a & ((1 << b) - 1))
                hi = lo + (1 << b)
                cosine, sine = row(cos_t, s, a, kk), row(sin_t, s, a, kk)
                term = grad[hi] * states[s, rows, lo * 128 : (lo + 1) * 128]
                term = term - grad[lo] * states[s, rows, hi * 128 : (hi + 1) * 128]
                tops[s - 7, a, pl.ds(kk, 1), :] = jnp.sum(term, axis=0, keepdims=True)
                grad[lo], grad[hi] = (
                    cosine * grad[lo] + sine * grad[hi],
                    cosine * grad[hi] - sine * grad[lo],
                )
        for s in (6, 5, 4, 3, 2, 1, 0):
            for t in range(8):
                other = lane_partner(grad[t], s)
                term = other * states[s, rows, t * 128 : (t + 1) * 128]
                terms[s, t, pl.ds(kk, 1), :] = jnp.sum(term, axis=0, keepdims=True)
                grad[t] = row(cos_t, s, t, kk) * grad[t] - row(sin_t, s, t, kk) * other
        for t in range(8):
            q_back[rows, t * 128 : (t + 1) * 128] = grad[t].astype(BF16)

        @pl.when(i < 15)
        def _():
            to = (kk % 8) * 2 + kk // 8
            remote(q_back.at[rows, :], out.at[own16, :], o_send, o_recv, (d, to)).start()

        @pl.when(i == 15)
        def _():
            out[own16, :] = q_back[rows, :]

    laid_out(7, 10)
    for s in range(7):
        sign = jnp.where((lane_col & (1 << s)) == 0, 1.0, -1.0)
        total = None
        for b in range(2):
            pick = jnp.where(lane_row == b * 64 + squeezed(lane_col, s), sign, 0.0)
            rows = jnp.concatenate([terms[s, 2 * a + b] for a in range(4)], axis=0)
            pick = pick.astype(BF16)
            for _ in range(3):
                high = rows.astype(BF16)
                part = jnp.dot(high, pick, preferred_element_type=F32)
                total = part if total is None else total + part
                rows = rows - high.astype(F32)
        for a in range(4):
            parts[s, :, a * 128 : (a + 1) * 128] = total[a * 16 : (a + 1) * 16]

    @pl.loop(0, 10)
    def _(i):
        to_section_owner((d + i) % 10)

    @pl.when(d < 14)
    def _():
        remote(by_tokens.at[0:15], by_tokens.at[0:15], p_send, p_recv, sibling).wait_recv()
        total = by_tokens[0]
        for i in range(1, 16):
            total = total + by_tokens[i]
        for j in range(16):
            row_out[j] = total[j : j + 1, :]

        @pl.loop(1, 16)
        def _(i):
            other = (slot + i) % 16
            remote(
                row_out.at[other], by_width.at[slot], r_send, r_recv, (d, (other % 8) * 2 + other // 8)
            ).start()

        by_width[slot] = row_out[slot]
        remote(by_width.at[0:15], by_width.at[0:15], r_send, r_recv, sibling).wait_recv()
        total = by_width[0]
        for i in range(1, 16):
            total = total + by_width[i]
        final[d] = total

        @pl.loop(1, 16)
        def _(i):
            remote(final.at[d], final.at[d], t_send, t_recv, ((d + i) % 16, k)).start()

        remote(final.at[0:13], final.at[0:13], t_send, t_recv, sibling).wait_recv()
        remote(by_tokens.at[0:13], by_tokens.at[0:13], p_send, p_recv, sibling).wait_send()
        remote(by_width.at[0:15], by_width.at[0:15], r_send, r_recv, sibling).wait_send()
        remote(final.at[0:15], final.at[0:15], t_send, t_recv, sibling).wait_send()

    @pl.when(d >= 14)
    def _():
        remote(final.at[0:14], final.at[0:14], t_send, t_recv, sibling).wait_recv()
        remote(by_tokens.at[0:14], by_tokens.at[0:14], p_send, p_recv, sibling).wait_send()

    for s in range(14):
        angle_out[s : s + 1, :] = final[s]

    remote(q_back.at[0:240], out.at[0:240], o_send, o_recv, sibling).wait()
    remote(ang.at[0, 0:7], ang.at[0, 0:7], g_send, g_recv, sibling).wait_send()
    remote(ang.at[0], ang.at[0], h_send, h_recv, sibling).wait_send()
    remote(steps, got_steps, s_send, s_recv.at[0], sibling).wait_send()
    remote(sent, got, d_send, d_recv.at[0], sibling).wait_send()
    remote(w_own, w_left, x_send.at[0], wl_sem.at[0], right).wait_send()
    remote(w_own, w_right, x_send.at[1], wr_sem.at[0], left).wait_send()
    half_rows = pl.ds(0, 512)
    remote(w_left.at[half_rows], w_far.at[half_rows], x_send.at[2], wf_sem.at[0], right).wait_send()
    remote(w_left.at[half_rows], w_far.at[half_rows], x_send.at[3], wf_sem.at[0], left).wait_send()
    for half in range(2):
        @pl.when(jnp.logical_not(jnp.logical_and(owner_y == y, c == half)))
        def _():
            ref = scaled.at[pl.ds(half * 128, 128), :]
            remote(ref, ref, b_send.at[half], b_recv.at[0], sibling).wait_send()
    for way in range(2):
        @pl.when(is_source)
        def _():
            remote(cots.at[0], cots.at[0], z_send.at[way], sib_sem.at[0], sibling).wait_send()

        @pl.when(jnp.logical_not(is_source))
        def _():
            ref = cots.at[0, 0:768, :]
            remote(ref, ref, z_send.at[way], sib_sem.at[0], sibling).wait_send()
    remote(cots.at[0:2], cots.at[0:2], z_send.at[2], sib_sem.at[0], sibling).wait_send()


VMEM = pl.BlockSpec(memory_space=pltpu.VMEM)
HBM = pl.BlockSpec(memory_space=pltpu.HBM)


def body(activations, angles, clip_bits, codes, exponents, cotangent):
    dma = pltpu.SemaphoreType.DMA
    return pl.pallas_call(
        all_kernel,
        out_shape=(
            jax.ShapeDtypeStruct((256, 1024), BF16),
            jax.ShapeDtypeStruct((14, 512), F32),
        ),
        in_specs=[HBM] * 6,
        out_specs=(VMEM,) * 2,
        scratch_shapes=[
            pltpu.VMEM((16, 1024), jnp.int32),
            pltpu.VMEM((1, 640), jnp.int32),
            pltpu.VMEM((256, 640), BF16),
            pltpu.VMEM((14, 512), F32),
            pltpu.VMEM((1024, 640), BF16),
            pltpu.VMEM((256, 640), BF16),
            pltpu.VMEM((4, 1024, 640), BF16),
            pltpu.VMEM((1024, 640), BF16),
            pltpu.VMEM((1024, 640), BF16),
            pltpu.VMEM((1024, 640), BF16),
            pltpu.VMEM((CHUNKS, 3, 256, CHUNK), jnp.int16),
            pltpu.VMEM((CHUNKS, 3, 256, CHUNK), jnp.int16),
            pltpu.VMEM((CHUNKS, 3, 1, 128), F32),
            pltpu.VMEM((CHUNKS, 3, 1, 128), F32),
            pltpu.VMEM((CHUNKS, 256, CHUNK), F32),
            pltpu.VMEM((CHUNKS, 256, CHUNK), BF16),
            pltpu.VMEM((256, 1024), BF16),
            pltpu.VMEM((256, 1024), BF16),
            pltpu.VMEM((2, 8, 16, 512), F32),
            pltpu.VMEM((14, 8, 16, 128), F32),
            pltpu.VMEM((14, 8, 16, 128), F32),
            pltpu.VMEM((14, 256, 1024), F32),
            pltpu.VMEM((7, 8, 16, 128), F32),
            pltpu.VMEM((7, 4, 16, 128), F32),
            pltpu.VMEM((256, 1024), F32),
            pltpu.VMEM((256, 1024), BF16),
            pltpu.VMEM((14, 16, 512), F32),
            pltpu.VMEM((16, 16, 512), F32),
            pltpu.VMEM((16, 1, 512), F32),
            pltpu.VMEM((16, 1, 512), F32),
            pltpu.VMEM((16, 1, 512), F32),
            dma((6,)), dma((4,)), dma((CHUNKS,)), dma((CHUNKS,)), dma((CHUNKS,)),
            dma((2,)), dma((4,)), dma((3,)), dma((4, 4)), dma((4, 4)), dma((4,)),
            dma, dma((CHUNKS,)), dma, dma((CHUNKS,)), dma, dma, dma, dma, dma, dma, dma, dma,
            dma, dma, dma, dma, dma, dma, dma, dma,
        ],
        compiler_params=pltpu.CompilerParams(
            collective_id=0, has_side_effects=True, vmem_limit_bytes=56 * 2**20
        ),
        cost_estimate=pl.CostEstimate(flops=5400000000, bytes_accessed=6000000, transcendentals=0),
    )(activations, clip_bits, codes, exponents[None, :], cotangent, angles)


def solution(mesh):
    placed = (
        P("dp", "tensor"),
        P(None, "tensor"),
        P("dp", "tensor"),
        P("tensor", "dp"),
        P(),
        P("dp", "tensor"),
    )
    return jax.shard_map(
        body,
        mesh=mesh,
        in_specs=placed,
        out_specs=(P("dp", "tensor"), P(None, "tensor")),
        check_vma=False,
    )
```

```python
import jax
import jax.numpy as jnp
from jax import lax
from jax.experimental import pallas as pl
from jax.experimental.pallas import tpu as pltpu
from jax.sharding import PartitionSpec as P

MESH = pl.DeviceIdType.MESH
F32 = jnp.float32
BF16 = jnp.bfloat16
CHUNK = 256
CHUNKS = 4
ORDER = (2, 1, 3, 0)


def place():
    d = lax.axis_index("dp")
    k = lax.axis_index("tensor")
    return d, k, d // 4, d % 4, k // 2, k % 2


def remote(src, dst, send, recv, to):
    return pltpu.make_async_remote_copy(
        src_ref=src, dst_ref=dst, send_sem=send, recv_sem=recv, device_id=to, device_id_type=MESH
    )


def sine_cosine(theta):
    h = theta * 0.5
    u = h * h
    s = 1.0 / 6227020800.0
    for term in (-1.0 / 39916800.0, 1.0 / 362880.0, -1.0 / 5040.0, 1.0 / 120.0, -1.0 / 6.0, 1.0):
        s = s * u + term
    s = s * h
    c = -1.0 / 87178291200.0
    for term in (1.0 / 479001600.0, -1.0 / 3628800.0, 1.0 / 40320.0, -1.0 / 720.0, 1.0 / 24.0, -0.5, 1.0):
        c = c * u + term
    return 2.0 * s * c, 1.0 - 2.0 * s * s


def squeezed(index, section):
    low = (1 << section) - 1
    return jnp.left_shift(jnp.right_shift(index, section + 1), section) | (index & low)


def lane_partner(value, section):
    lanes = lax.broadcasted_iota(jnp.int32, value.shape, 1)
    return jnp.take_along_axis(value, lanes ^ (1 << section), axis=1, mode="promise_in_bounds")


def pair_bit(section):
    return 8 if section == 10 else 1 << (section - 11)


def pairs_of(section):
    bit = pair_bit(section)
    pairs = []
    for m in range(8):
        b = section - 10
        lower = ((m >> b) << (b + 1)) | (m & ((1 << b) - 1))
        s0 = (lower % 2) * 8 + lower // 2
        pairs.append((m, s0, s0 + bit))
    return pairs


def all_kernel(
    acts, clip, codes, exps, cot, angles,
    out, angle_out,
    clip_v, exps_v, cot_v, ang_v, w_own,
    scaled, cots, w_left, w_right, w_far, sent, got, steps, got_steps, whole, narrow,
    q_in, a_in, ang, cos_t, sin_t, states, terms, tops, tall, q_back,
    parts, by_tokens, row_out, by_width, final,
    l_sem, x_send, wl_sem, wr_sem, wf_sem, b_send, b_recv, own_send, z_send, up_sem, down_sem, sib_sem,
    s_send, s_recv, d_send, d_recv, e_send, e_recv, f_send, f_recv, g_send, g_recv, h_send, h_recv,
    o_send, o_recv, p_send, p_recv, r_send, r_recv, t_send, t_recv,
):
    d, k, x, y, z, c = place()
    slot = c * 8 + z
    mine16 = pl.ds(pl.multiple_of(slot * 16, 16), 16)
    own16 = pl.ds(pl.multiple_of(k * 16, 16), 16)

    def dev(px, py, pz, pc):
        return (px * 4 + py, pz * 2 + pc)

    right = dev((x + 1) % 4, y, z, c)
    left = dev((x + 3) % 4, y, z, c)
    up = dev(x, y, (z + 1) % 8, c)
    down = dev(x, y, (z + 7) % 8, c)
    sibling = dev(x, y, z, 1 - c)

    loads = [
        pltpu.make_async_copy(cot, cot_v, l_sem.at[0]),
        pltpu.make_async_copy(exps.at[:, pl.ds(pl.multiple_of(k * 640, 128), 640)], exps_v, l_sem.at[1]),
        pltpu.make_async_copy(angles, ang_v, l_sem.at[2]),
        pltpu.make_async_copy(codes, w_own, l_sem.at[3]),
        pltpu.make_async_copy(clip, clip_v, l_sem.at[4]),
    ]
    own_copy = pltpu.make_async_copy(acts.at[own16, :], a_in.at[mine16, :], l_sem.at[5])
    barrier = pltpu.get_barrier_semaphore()

    def greet(to):
        pl.semaphore_signal(barrier, inc=1, device_id=to, device_id_type=MESH)

    for copy in loads:
        copy.start()
    own_copy.start()

    @pl.loop(1, 16)
    def _(i):
        greet((d, (k + i) % 16))
        greet(((d + i) % 16, k))

    for step in range(1, 4):
        greet(dev(x, (y + step) % 4, z, 1 - c))
    pl.semaphore_wait(barrier, 33)

    def send_activations():
        @pl.loop(1, 16)
        def _(i):
            to = (k + i) % 16
            remote(
                acts.at[pl.ds(pl.multiple_of(to * 16, 16), 16), :], a_in.at[mine16, :], f_send, f_recv, (d, to)
            ).start()

    def send_codes(f):
        rows = pl.ds(f * CHUNK, CHUNK)
        remote(codes.at[rows], w_left.at[rows], x_send.at[0], wl_sem.at[f], right).start()
        remote(codes.at[rows], w_right.at[rows], x_send.at[1], wr_sem.at[f], left).start()

    send_codes(0)
    send_codes(1)

    for n in range(3):
        loads[n].wait()
    minus = -exps_v[...]
    scale = jnp.ones((1, 640), F32)
    for bit in range(5):
        on = jnp.bitwise_and(jnp.right_shift(minus, bit), 1) == 1
        scale = jnp.where(on, scale * (2.0 ** -(2**bit)), scale)
    scaled[...] = (cot_v[...].astype(F32) * scale).astype(BF16)

    def piece(part, token_group, half):
        start = pl.multiple_of(token_group * 256 + half * 128, 128)
        return cots.at[part, pl.ds(start, 128), :]

    owner_y = k % 4
    for half in range(2):
        mine = jnp.logical_and(owner_y == y, c == half)

        @pl.when(mine)
        def _():
            start = pl.multiple_of(y * 256 + half * 128, 128)
            cots[z // 2, pl.ds(start, 128), :] = scaled[half * 128 : (half + 1) * 128, :]

        @pl.when(jnp.logical_not(mine))
        def _():
            remote(
                scaled.at[pl.ds(half * 128, 128), :],
                piece(z // 2, y, half),
                b_send.at[half],
                b_recv.at[y],
                dev(x, owner_y, z, half),
            ).start()

    ang[c, z, 0:14, :] = ang_v[...]
    ang[c, z, 14:16, :] = jnp.zeros((2, 512), F32)

    @pl.loop(1, 8)
    def _(i):
        remote(
            ang.at[c, z], ang.at[c, z], g_send, g_recv, (d, ((z + i) % 8) * 2 + c)
        ).start()

    def to_sibling(ref, n):
        remote(ref, ref, z_send.at[2], sib_sem.at[n], sibling).start()

    is_source = (z % 2) == (y // 2)

    def group(n):
        return (y + ORDER[n]) % 4

    def own_copies(n):
        ref = piece(z // 2, group(n), c)
        return (
            remote(ref, ref, own_send.at[0, n], up_sem.at[0, n], up),
            remote(ref, ref, own_send.at[1, n], down_sem.at[0, n], down),
        )

    def send_own(n):
        g = group(n)
        ref = piece(z // 2, g, c)

        @pl.when(jnp.logical_not(jnp.logical_and(y == g, y % 2 == c)))
        def _():
            remote(ref, ref, b_send.at[0], b_recv.at[g], sibling).wait_recv()

        if n > 0:
            for copy in own_copies(n - 1):
                copy.wait_send()
        for copy in own_copies(n):
            copy.start()
        to_sibling(ref, n)

    @pl.when(is_source)
    def _():
        for n in range(3):
            send_own(n)

    def pass_on(t, n):
        below = (z + 8 - t) % 8
        above = (z + t) % 8

        @pl.when((below % 2) == (y // 2))
        def _():
            if t < 4 or n % 2 == 0:
                ref = piece(below // 2, group(n), c)
                remote(ref, ref, z_send.at[0], up_sem.at[t - 1, n], up).wait_recv()
                if t < 3 or (t == 3 and n % 2 == 0):
                    remote(ref, ref, z_send.at[0], up_sem.at[t, n], up).start()
                to_sibling(ref, n)
            if t < 4 or n % 2 == 1:
                ref = piece(above // 2, group(n), c)
                remote(ref, ref, z_send.at[1], down_sem.at[t - 1, n], down).wait_recv()
                if t < 3 or (t == 3 and n % 2 == 1):
                    remote(ref, ref, z_send.at[1], down_sem.at[t, n], down).start()
                to_sibling(ref, n)

    def group_here(n):
        remote(cots.at[0, 0:512, :], cots.at[0, 0:512, :], z_send.at[2], sib_sem.at[n], sibling).wait_recv()

    def forward(f):
        rows = pl.ds(f * CHUNK, CHUNK)
        if f % 2 == 0:
            remote(w_left.at[rows], w_left.at[rows], x_send.at[0], wl_sem.at[f], right).wait_recv()
            remote(w_left.at[rows], w_far.at[rows], x_send.at[2], wf_sem.at[f], right).start()
        else:
            remote(w_right.at[rows], w_right.at[rows], x_send.at[1], wr_sem.at[f], left).wait_recv()
            remote(w_right.at[rows], w_far.at[rows], x_send.at[3], wf_sem.at[f], left).start()

    def chunk_here(f):
        rows = pl.ds(f * CHUNK, CHUNK)
        if f % 2 == 1:
            remote(w_left.at[rows], w_left.at[rows], x_send.at[0], wl_sem.at[f], right).wait_recv()
        else:
            remote(w_right.at[rows], w_right.at[rows], x_send.at[1], wr_sem.at[f], left).wait_recv()
        remote(w_far.at[rows], w_far.at[rows], x_send.at[2], wf_sem.at[f], right).wait_recv()

    def product(f, n):
        rows = pl.ds(pl.multiple_of(f * CHUNK, CHUNK), CHUNK)
        to_y = (y + jnp.where(n == 3, 0, jnp.where(n == 0, 2, jnp.where(n == 1, 1, 3)))) % 4
        tokens = pl.ds(pl.multiple_of(to_y * 256, 256), 256)

        def part(index, ref):
            return lax.dot_general(
                cots[index, tokens, :], ref[rows, :], (((1,), (1,)), ((), ())),
                preferred_element_type=F32,
            )

        total = part(x, w_own)
        total = total + part((x + 3) % 4, w_left)
        total = total + part((x + 1) % 4, w_right)
        return to_y, total + part((x + 2) % 4, w_far)

    def to_row(f, n):
        to_y, total = product(f, n)
        most = jnp.max(jnp.max(jnp.abs(total), axis=0, keepdims=True), axis=1, keepdims=True)
        most = jnp.maximum(most, 1e-30)
        sent[f, n] = jnp.round(total * (32000.0 / most)).astype(jnp.int32).astype(jnp.int16)
        steps[f, n] = jnp.broadcast_to(most * (1.0 / 32000.0), (1, 128))
        remote(steps.at[f, n], got_steps.at[f, n], s_send, s_recv.at[f], dev(x, to_y, z, c)).start()
        remote(sent.at[f, n], got.at[f, n], d_send, d_recv.at[f], dev(x, to_y, z, c)).start()

    lane_row = lax.broadcasted_iota(jnp.int32, (128, 128), 1)
    lane_col = lax.broadcasted_iota(jnp.int32, (128, 128), 0)

    def low_tables(first, last):
        for s in range(first, last):
            rows = jnp.concatenate(
                [ang[core, :, s, a * 128 : (a + 1) * 128] for a in range(4) for core in range(2)], axis=0
            )
            for b in range(2):
                pick = jnp.where(lane_col == b * 64 + squeezed(lane_row, s), 1.0, 0.0)
                theta = jnp.dot(rows, pick, precision=lax.Precision.HIGHEST, preferred_element_type=F32)
                sine, cosine = sine_cosine(theta)
                upper = (lax.broadcasted_iota(jnp.int32, theta.shape, 1) & (1 << s)) != 0
                signed = jnp.where(upper, sine, -sine)
                for a in range(4):
                    cos_t[s, 2 * a + b] = cosine[a * 16 : (a + 1) * 16]
                    sin_t[s, 2 * a + b] = signed[a * 16 : (a + 1) * 16]

    def high_tables():
        for s in range(7, 14):
            for a in range(4):
                for core in range(2):
                    sine, cosine = sine_cosine(ang[core, :, s, a * 128 : (a + 1) * 128])
                    cos_t[s, a, core * 8 : core * 8 + 8] = cosine
                    sin_t[s, a, core * 8 : core * 8 + 8] = sine

    pass_on(1, 0)
    pass_on(2, 0)

    @pl.when(is_source)
    def _():
        send_own(3)

    pass_on(1, 1)
    forward(0)
    forward(1)
    pass_on(3, 0)
    remote(ang.at[0, 0:7], ang.at[0, 0:7], g_send, g_recv, sibling).wait_recv()
    remote(ang.at[c], ang.at[c], h_send, h_recv, sibling).start()
    send_codes(2)
    pass_on(2, 1)
    send_codes(3)
    pass_on(4, 0)
    pass_on(1, 2)
    remote(ang.at[0], ang.at[0], h_send, h_recv, sibling).wait_recv()
    pass_on(3, 1)
    loads[3].wait()
    loads[4].wait()
    own_copy.wait()
    pass_on(2, 2)
    group_here(0)
    chunk_here(0)
    to_row(0, 0)
    pass_on(4, 1)
    chunk_here(1)
    to_row(1, 0)
    pass_on(1, 3)
    low_tables(0, 2)
    pass_on(3, 2)
    group_here(1)

    @pl.loop(0, 2)
    def _(f):
        to_row(f, 1)

    forward(2)
    pass_on(2, 3)
    forward(3)
    low_tables(2, 4)
    pass_on(4, 2)
    pass_on(3, 3)
    send_activations()
    group_here(2)

    @pl.loop(0, 2)
    def _(f):
        to_row(f, 2)

    chunk_here(2)

    @pl.loop(0, 3)
    def _(n):
        to_row(2, n)

    pass_on(4, 3)
    low_tables(4, 7)
    chunk_here(3)

    @pl.loop(0, 3)
    def _(n):
        to_row(3, n)

    high_tables()
    group_here(3)

    def finish(f):
        lanes = pl.ds(pl.multiple_of(f * CHUNK, CHUNK), CHUNK)
        remote(steps.at[f], got_steps.at[f], s_send, s_recv.at[f], sibling).wait_recv()
        remote(got.at[f], got.at[f], d_send, d_recv.at[f], sibling).wait_recv()
        place_in_word = lax.broadcasted_iota(jnp.int32, (16, CHUNK), 0)

        def masked(w):
            rows = pl.ds(pl.multiple_of(w * 16, 16), 16)
            total = whole[f, rows, :]
            for j in range(3):
                step = jnp.concatenate([got_steps[f, j], got_steps[f, j]], axis=1)
                total = total + got[f, j, rows, :].astype(jnp.int32).astype(F32) * step
            word = jnp.broadcast_to(clip_v[pl.ds(w, 1), lanes], (16, CHUNK))
            bit = jnp.bitwise_and(jnp.right_shift(word, place_in_word), 1)
            return rows, jnp.where(bit == 1, total, 0.0)

        @pl.loop(1, 16)
        def _(i):
            to = (k + i) % 16
            rows, value = masked(to)
            narrow[f, rows, :] = value.astype(BF16)
            remote(
                narrow.at[f, rows, :], q_in.at[mine16, lanes], e_send, e_recv, (d, to)
            ).start()

        _, value = masked(k)
        q_in[mine16, lanes] = value.astype(BF16)

    @pl.loop(0, CHUNKS)
    def _(f):
        _, total = product(f, 3)
        whole[f] = total
        finish(f)

    remote(a_in.at[0:240], a_in.at[0:240], f_send, f_recv, sibling).wait()

    def row(table, s, tile, index):
        return jnp.broadcast_to(table[s, tile, pl.ds(index, 1), :], (16, 128))

    @pl.loop(0, 16)
    def _(kk):
        rows = pl.ds(pl.multiple_of(kk * 16, 16), 16)
        field = [a_in[rows, t * 128 : (t + 1) * 128].astype(F32) for t in range(8)]
        for s in range(7):
            for t in range(8):
                field[t] = row(cos_t, s, t, kk) * field[t] + row(sin_t, s, t, kk) * lane_partner(field[t], s)
                states[s, rows, t * 128 : (t + 1) * 128] = field[t]
        for s in range(7, 10):
            b = s - 7
            for a in range(4):
                lo = ((a >> b) << (b + 1)) | (a & ((1 << b) - 1))
                hi = lo + (1 << b)
                cosine, sine = row(cos_t, s, a, kk), row(sin_t, s, a, kk)
                field[lo], field[hi] = (
                    cosine * field[lo] - sine * field[hi],
                    sine * field[lo] + cosine * field[hi],
                )
            for t in range(8):
                states[s, rows, t * 128 : (t + 1) * 128] = field[t]

    def fixed_row(table, s, t, m):
        return jnp.broadcast_to(table[s, t % 4, pl.ds((t // 4) * 8 + m, 1), :], (16, 128))

    def halves(lo, hi):
        yield slice(lo * 16, lo * 16 + 16), slice(hi * 16, hi * 16 + 16)

    @pl.loop(0, 8)
    def _(t):
        lanes = pl.ds(pl.multiple_of(t * 128, 128), 128)
        for s in range(10, 14):
            for m, lo, hi in pairs_of(s):
                cosine, sine = fixed_row(cos_t, s, t, m), fixed_row(sin_t, s, t, m)
                for lo_rows, hi_rows in halves(lo, hi):
                    v_lo, v_hi = states[s - 1, lo_rows, lanes], states[s - 1, hi_rows, lanes]
                    states[s, lo_rows, lanes] = cosine * v_lo - sine * v_hi
                    states[s, hi_rows, lanes] = sine * v_lo + cosine * v_hi

    remote(q_in.at[0:240], q_in.at[0:240], e_send, e_recv, sibling).wait()

    def to_section_owner(s):
        @pl.when(d != s)
        def _():
            remote(parts.at[s], by_tokens.at[d], p_send, p_recv, (s, k)).start()

        @pl.when(d == s)
        def _():
            by_tokens[d] = parts[s]

    @pl.loop(0, 8)
    def _(t):
        lanes = pl.ds(pl.multiple_of(t * 128, 128), 128)
        for s in (13, 12, 11, 10):
            source = q_in if s == 13 else tall
            for m, lo, hi in pairs_of(s):
                cosine, sine = fixed_row(cos_t, s, t, m), fixed_row(sin_t, s, t, m)
                total = None
                for lo_rows, hi_rows in halves(lo, hi):
                    q_lo, q_hi = source[lo_rows, lanes].astype(F32), source[hi_rows, lanes].astype(F32)
                    term = q_hi * states[s, lo_rows, lanes] - q_lo * states[s, hi_rows, lanes]
                    total = term if total is None else total + term
                    tall[lo_rows, lanes] = cosine * q_lo + sine * q_hi
                    tall[hi_rows, lanes] = cosine * q_hi - sine * q_lo
                tops[s - 7, t % 4, pl.ds((t // 4) * 8 + m, 1), :] = jnp.sum(total, axis=0, keepdims=True)

    def laid_out(first, last):
        for s in range(first, last):
            for a in range(4):
                parts[s, :, a * 128 : (a + 1) * 128] = tops[s - 7, a]

    laid_out(10, 14)

    @pl.loop(0, 4)
    def _(i):
        to_section_owner(10 + (d + i) % 4)

    @pl.loop(0, 16)
    def _(i):
        kk = (slot + 1 + i) % 16
        rows = pl.ds(pl.multiple_of(kk * 16, 16), 16)
        grad = [tall[rows, t * 128 : (t + 1) * 128] for t in range(8)]
        for s in (9, 8, 7):
            b = s - 7
            for a in range(4):
                lo = ((a >> b) << (b + 1)) | (a & ((1 << b) - 1))
                hi = lo + (1 << b)
                cosine, sine = row(cos_t, s, a, kk), row(sin_t, s, a, kk)
                term = grad[hi] * states[s, rows, lo * 128 : (lo + 1) * 128]
                term = term - grad[lo] * states[s, rows, hi * 128 : (hi + 1) * 128]
                tops[s - 7, a, pl.ds(kk, 1), :] = jnp.sum(term, axis=0, keepdims=True)
                grad[lo], grad[hi] = (
                    cosine * grad[lo] + sine * grad[hi],
                    cosine * grad[hi] - sine * grad[lo],
                )
        for s in (6, 5, 4, 3, 2, 1, 0):
            for t in range(8):
                other = lane_partner(grad[t], s)
                term = other * states[s, rows, t * 128 : (t + 1) * 128]
                terms[s, t, pl.ds(kk, 1), :] = jnp.sum(term, axis=0, keepdims=True)
                grad[t] = row(cos_t, s, t, kk) * grad[t] - row(sin_t, s, t, kk) * other
        for t in range(8):
            q_back[rows, t * 128 : (t + 1) * 128] = grad[t].astype(BF16)

        @pl.when(i < 15)
        def _():
            to = (kk % 8) * 2 + kk // 8
            remote(q_back.at[rows, :], out.at[own16, :], o_send, o_recv, (d, to)).start()

        @pl.when(i == 15)
        def _():
            out[own16, :] = q_back[rows, :]

    laid_out(7, 10)
    for s in range(7):
        sign = jnp.where((lane_col & (1 << s)) == 0, 1.0, -1.0)
        total = None
        for b in range(2):
            pick = jnp.where(lane_row == b * 64 + squeezed(lane_col, s), sign, 0.0)
            rows = jnp.concatenate([terms[s, 2 * a + b] for a in range(4)], axis=0)
            pick = pick.astype(BF16)
            for _ in range(3):
                high = rows.astype(BF16)
                part = jnp.dot(high, pick, preferred_element_type=F32)
                total = part if total is None else total + part
                rows = rows - high.astype(F32)
        for a in range(4):
            parts[s, :, a * 128 : (a + 1) * 128] = total[a * 16 : (a + 1) * 16]

    @pl.loop(0, 10)
    def _(i):
        to_section_owner((d + i) % 10)

    @pl.when(d < 14)
    def _():
        remote(by_tokens.at[0:15], by_tokens.at[0:15], p_send, p_recv, sibling).wait_recv()
        total = by_tokens[0]
        for i in range(1, 16):
            total = total + by_tokens[i]
        for j in range(16):
            row_out[j] = total[j : j + 1, :]

        @pl.loop(1, 16)
        def _(i):
            other = (slot + i) % 16
            remote(
                row_out.at[other], by_width.at[slot], r_send, r_recv, (d, (other % 8) * 2 + other // 8)
            ).start()

        by_width[slot] = row_out[slot]
        remote(by_width.at[0:15], by_width.at[0:15], r_send, r_recv, sibling).wait_recv()
        total = by_width[0]
        for i in range(1, 16):
            total = total + by_width[i]
        final[d] = total

        @pl.loop(1, 16)
        def _(i):
            remote(final.at[d], final.at[d], t_send, t_recv, ((d + i) % 16, k)).start()

        remote(final.at[0:13], final.at[0:13], t_send, t_recv, sibling).wait_recv()
        remote(by_tokens.at[0:13], by_tokens.at[0:13], p_send, p_recv, sibling).wait_send()
        remote(by_width.at[0:15], by_width.at[0:15], r_send, r_recv, sibling).wait_send()
        remote(final.at[0:15], final.at[0:15], t_send, t_recv, sibling).wait_send()

    @pl.when(d >= 14)
    def _():
        remote(final.at[0:14], final.at[0:14], t_send, t_recv, sibling).wait_recv()
        remote(by_tokens.at[0:14], by_tokens.at[0:14], p_send, p_recv, sibling).wait_send()

    for s in range(14):
        angle_out[s : s + 1, :] = final[s]

    remote(q_back.at[0:240], out.at[0:240], o_send, o_recv, sibling).wait()
    remote(ang.at[0, 0:7], ang.at[0, 0:7], g_send, g_recv, sibling).wait_send()
    remote(ang.at[0], ang.at[0], h_send, h_recv, sibling).wait_send()
    remote(steps, got_steps, s_send, s_recv.at[0], sibling).wait_send()
    remote(sent, got, d_send, d_recv.at[0], sibling).wait_send()
    remote(w_own, w_left, x_send.at[0], wl_sem.at[0], right).wait_send()
    remote(w_own, w_right, x_send.at[1], wr_sem.at[0], left).wait_send()
    half_rows = pl.ds(0, 512)
    remote(w_left.at[half_rows], w_far.at[half_rows], x_send.at[2], wf_sem.at[0], right).wait_send()
    remote(w_left.at[half_rows], w_far.at[half_rows], x_send.at[3], wf_sem.at[0], left).wait_send()
    for half in range(2):
        @pl.when(jnp.logical_not(jnp.logical_and(owner_y == y, c == half)))
        def _():
            ref = scaled.at[pl.ds(half * 128, 128), :]
            remote(ref, ref, b_send.at[half], b_recv.at[0], sibling).wait_send()
    for way in range(2):
        @pl.when(is_source)
        def _():
            ref = cots.at[0, 0:512, :]
            remote(ref, ref, z_send.at[way], sib_sem.at[0], sibling).wait_send()
            own_copies(3)[way].wait_send()

        @pl.when(jnp.logical_not(is_source))
        def _():
            ref = cots.at[0, 0:768, :]
            remote(ref, ref, z_send.at[way], sib_sem.at[0], sibling).wait_send()
    remote(cots.at[0:2], cots.at[0:2], z_send.at[2], sib_sem.at[0], sibling).wait_send()


VMEM = pl.BlockSpec(memory_space=pltpu.VMEM)
HBM = pl.BlockSpec(memory_space=pltpu.HBM)


def body(activations, angles, clip_bits, codes, exponents, cotangent):
    dma = pltpu.SemaphoreType.DMA
    return pl.pallas_call(
        all_kernel,
        out_shape=(
            jax.ShapeDtypeStruct((256, 1024), BF16),
            jax.ShapeDtypeStruct((14, 512), F32),
        ),
        in_specs=[HBM] * 6,
        out_specs=(VMEM,) * 2,
        scratch_shapes=[
            pltpu.VMEM((16, 1024), jnp.int32),
            pltpu.VMEM((1, 640), jnp.int32),
            pltpu.VMEM((256, 640), BF16),
            pltpu.VMEM((14, 512), F32),
            pltpu.VMEM((1024, 640), BF16),
            pltpu.VMEM((256, 640), BF16),
            pltpu.VMEM((4, 1024, 640), BF16),
            pltpu.VMEM((1024, 640), BF16),
            pltpu.VMEM((1024, 640), BF16),
            pltpu.VMEM((1024, 640), BF16),
            pltpu.VMEM((CHUNKS, 3, 256, CHUNK), jnp.int16),
            pltpu.VMEM((CHUNKS, 3, 256, CHUNK), jnp.int16),
            pltpu.VMEM((CHUNKS, 3, 1, 128), F32),
            pltpu.VMEM((CHUNKS, 3, 1, 128), F32),
            pltpu.VMEM((CHUNKS, 256, CHUNK), F32),
            pltpu.VMEM((CHUNKS, 256, CHUNK), BF16),
            pltpu.VMEM((256, 1024), BF16),
            pltpu.VMEM((256, 1024), BF16),
            pltpu.VMEM((2, 8, 16, 512), F32),
            pltpu.VMEM((14, 8, 16, 128), F32),
            pltpu.VMEM((14, 8, 16, 128), F32),
            pltpu.VMEM((14, 256, 1024), F32),
            pltpu.VMEM((7, 8, 16, 128), F32),
            pltpu.VMEM((7, 4, 16, 128), F32),
            pltpu.VMEM((256, 1024), F32),
            pltpu.VMEM((256, 1024), BF16),
            pltpu.VMEM((14, 16, 512), F32),
            pltpu.VMEM((16, 16, 512), F32),
            pltpu.VMEM((16, 1, 512), F32),
            pltpu.VMEM((16, 1, 512), F32),
            pltpu.VMEM((16, 1, 512), F32),
            dma((6,)), dma((4,)), dma((CHUNKS,)), dma((CHUNKS,)), dma((CHUNKS,)),
            dma((2,)), dma((4,)), dma((2, 4)), dma((3,)), dma((4, 4)), dma((4, 4)), dma((4,)),
            dma, dma((CHUNKS,)), dma, dma((CHUNKS,)), dma, dma, dma, dma, dma, dma, dma, dma,
            dma, dma, dma, dma, dma, dma, dma, dma,
        ],
        compiler_params=pltpu.CompilerParams(
            collective_id=0, has_side_effects=True, vmem_limit_bytes=56 * 2**20
        ),
        cost_estimate=pl.CostEstimate(flops=5400000000, bytes_accessed=6000000, transcendentals=0),
    )(activations, clip_bits, codes, exponents[None, :], cotangent, angles)


def solution(mesh):
    placed = (
        P("dp", "tensor"),
        P(None, "tensor"),
        P("dp", "tensor"),
        P("tensor", "dp"),
        P(),
        P("dp", "tensor"),
    )
    return jax.shard_map(
        body,
        mesh=mesh,
        in_specs=placed,
        out_specs=(P("dp", "tensor"), P(None, "tensor")),
        check_vma=False,
    )
```

```python
import jax
import jax.numpy as jnp
from jax import lax
from jax.experimental import pallas as pl
from jax.experimental.pallas import tpu as pltpu
from jax.sharding import PartitionSpec as P

MESH = pl.DeviceIdType.MESH
F32 = jnp.float32
BF16 = jnp.bfloat16
CHUNK = 256
CHUNKS = 4
ORDER = (2, 1, 3, 0)


def place():
    d = lax.axis_index("dp")
    k = lax.axis_index("tensor")
    return d, k, d // 4, d % 4, k // 2, k % 2


def remote(src, dst, send, recv, to):
    return pltpu.make_async_remote_copy(
        src_ref=src, dst_ref=dst, send_sem=send, recv_sem=recv, device_id=to, device_id_type=MESH
    )


def sine_cosine(theta):
    h = theta * 0.5
    u = h * h
    s = 1.0 / 6227020800.0
    for term in (-1.0 / 39916800.0, 1.0 / 362880.0, -1.0 / 5040.0, 1.0 / 120.0, -1.0 / 6.0, 1.0):
        s = s * u + term
    s = s * h
    c = -1.0 / 87178291200.0
    for term in (1.0 / 479001600.0, -1.0 / 3628800.0, 1.0 / 40320.0, -1.0 / 720.0, 1.0 / 24.0, -0.5, 1.0):
        c = c * u + term
    return 2.0 * s * c, 1.0 - 2.0 * s * s


def squeezed(index, section):
    low = (1 << section) - 1
    return jnp.left_shift(jnp.right_shift(index, section + 1), section) | (index & low)


def lane_partner(value, section):
    lanes = lax.broadcasted_iota(jnp.int32, value.shape, 1)
    return jnp.take_along_axis(value, lanes ^ (1 << section), axis=1, mode="promise_in_bounds")


def pair_bit(section):
    return 8 if section == 10 else 1 << (section - 11)


def pairs_of(section):
    bit = pair_bit(section)
    pairs = []
    for m in range(8):
        b = section - 10
        lower = ((m >> b) << (b + 1)) | (m & ((1 << b) - 1))
        s0 = (lower % 2) * 8 + lower // 2
        pairs.append((m, s0, s0 + bit))
    return pairs


def all_kernel(
    acts, clip, codes, exps, cot, angles,
    out, angle_out,
    clip_v, exps_v, cot_v, ang_v, w_own,
    scaled, cots, w_left, w_right, w_far, sent, got, steps, got_steps, whole, narrow,
    q_in, a_in, ang, cos_t, sin_t, states, terms, tops, tall, q_back,
    parts, by_tokens, row_out, by_width, final,
    l_sem, x_send, wl_sem, wr_sem, wf_sem, b_send, b_recv, own_send, z_send, up_sem, down_sem, sib_sem,
    s_send, s_recv, d_send, d_recv, e_send, e_recv, f_send, f_recv, g_send, g_recv, h_send, h_recv,
    o_send, o_recv, p_send, p_recv, r_send, r_recv, t_send, t_recv,
):
    d, k, x, y, z, c = place()
    slot = c * 8 + z
    mine16 = pl.ds(pl.multiple_of(slot * 16, 16), 16)
    own16 = pl.ds(pl.multiple_of(k * 16, 16), 16)

    def dev(px, py, pz, pc):
        return (px * 4 + py, pz * 2 + pc)

    right = dev((x + 1) % 4, y, z, c)
    left = dev((x + 3) % 4, y, z, c)
    up = dev(x, y, (z + 1) % 8, c)
    down = dev(x, y, (z + 7) % 8, c)
    sibling = dev(x, y, z, 1 - c)

    loads = [
        pltpu.make_async_copy(cot, cot_v, l_sem.at[0]),
        pltpu.make_async_copy(exps.at[:, pl.ds(pl.multiple_of(k * 640, 128), 640)], exps_v, l_sem.at[1]),
        pltpu.make_async_copy(angles, ang_v, l_sem.at[2]),
        pltpu.make_async_copy(codes, w_own, l_sem.at[3]),
        pltpu.make_async_copy(clip, clip_v, l_sem.at[4]),
    ]
    own_copy = pltpu.make_async_copy(acts.at[own16, :], a_in.at[mine16, :], l_sem.at[5])
    barrier = pltpu.get_barrier_semaphore()

    def greet(to):
        pl.semaphore_signal(barrier, inc=1, device_id=to, device_id_type=MESH)

    for copy in loads:
        copy.start()
    own_copy.start()

    @pl.loop(1, 16)
    def _(i):
        greet((d, (k + i) % 16))
        greet(((d + i) % 16, k))

    for step in range(1, 4):
        greet(dev(x, (y + step) % 4, z, 1 - c))
    pl.semaphore_wait(barrier, 33)

    def send_activations():
        @pl.loop(1, 16)
        def _(i):
            to = (k + i) % 16
            remote(
                acts.at[pl.ds(pl.multiple_of(to * 16, 16), 16), :], a_in.at[mine16, :], f_send, f_recv, (d, to)
            ).start()

    def send_codes(f):
        rows = pl.ds(f * CHUNK, CHUNK)
        remote(codes.at[rows], w_left.at[rows], x_send.at[0], wl_sem.at[f], right).start()
        remote(codes.at[rows], w_right.at[rows], x_send.at[1], wr_sem.at[f], left).start()

    send_codes(0)
    send_codes(1)

    for n in range(3):
        loads[n].wait()
    minus = -exps_v[...]
    scale = jnp.ones((1, 640), F32)
    for bit in range(5):
        on = jnp.bitwise_and(jnp.right_shift(minus, bit), 1) == 1
        scale = jnp.where(on, scale * (2.0 ** -(2**bit)), scale)
    scaled[...] = (cot_v[...].astype(F32) * scale).astype(BF16)

    def piece(part, token_group, half):
        start = pl.multiple_of(token_group * 256 + half * 128, 128)
        return cots.at[part, pl.ds(start, 128), :]

    owner_y = k % 4
    for half in range(2):
        mine = jnp.logical_and(owner_y == y, c == half)

        @pl.when(mine)
        def _():
            start = pl.multiple_of(y * 256 + half * 128, 128)
            cots[z // 2, pl.ds(start, 128), :] = scaled[half * 128 : (half + 1) * 128, :]

        @pl.when(jnp.logical_not(mine))
        def _():
            remote(
                scaled.at[pl.ds(half * 128, 128), :],
                piece(z // 2, y, half),
                b_send.at[half],
                b_recv.at[y],
                dev(x, owner_y, z, half),
            ).start()

    ang[c, z, 0:14, :] = ang_v[...]
    ang[c, z, 14:16, :] = jnp.zeros((2, 512), F32)

    @pl.loop(1, 8)
    def _(i):
        remote(
            ang.at[c, z], ang.at[c, z], g_send, g_recv, (d, ((z + i) % 8) * 2 + c)
        ).start()

    def to_sibling(ref, n):
        remote(ref, ref, z_send.at[2], sib_sem.at[n], sibling).start()

    is_source = (z % 2) == (y // 2)

    def group(n):
        return (y + ORDER[n]) % 4

    def own_copies(n):
        ref = piece(z // 2, group(n), c)
        return (
            remote(ref, ref, own_send.at[0, n], up_sem.at[0, n], up),
            remote(ref, ref, own_send.at[1, n], down_sem.at[0, n], down),
        )

    def send_own(n):
        g = group(n)
        ref = piece(z // 2, g, c)

        @pl.when(jnp.logical_not(jnp.logical_and(y == g, y % 2 == c)))
        def _():
            remote(ref, ref, b_send.at[0], b_recv.at[g], sibling).wait_recv()

        if n > 0:
            for copy in own_copies(n - 1):
                copy.wait_send()
        for copy in own_copies(n):
            copy.start()
        to_sibling(ref, n)

    @pl.when(is_source)
    def _():
        for n in range(3):
            send_own(n)

    def pass_on(t, n):
        below = (z + 8 - t) % 8
        above = (z + t) % 8

        @pl.when((below % 2) == (y // 2))
        def _():
            if t < 4 or n % 2 == 0:
                ref = piece(below // 2, group(n), c)
                remote(ref, ref, z_send.at[0], up_sem.at[t - 1, n], up).wait_recv()
                if t < 3 or (t == 3 and n % 2 == 0):
                    remote(ref, ref, z_send.at[0], up_sem.at[t, n], up).start()
                to_sibling(ref, n)
            if t < 4 or n % 2 == 1:
                ref = piece(above // 2, group(n), c)
                remote(ref, ref, z_send.at[1], down_sem.at[t - 1, n], down).wait_recv()
                if t < 3 or (t == 3 and n % 2 == 1):
                    remote(ref, ref, z_send.at[1], down_sem.at[t, n], down).start()
                to_sibling(ref, n)

    def group_here(n):
        remote(cots.at[0, 0:512, :], cots.at[0, 0:512, :], z_send.at[2], sib_sem.at[n], sibling).wait_recv()

    def forward(f):
        rows = pl.ds(f * CHUNK, CHUNK)
        if f % 2 == 0:
            remote(w_left.at[rows], w_left.at[rows], x_send.at[0], wl_sem.at[f], right).wait_recv()
            remote(w_left.at[rows], w_far.at[rows], x_send.at[2], wf_sem.at[f], right).start()
        else:
            remote(w_right.at[rows], w_right.at[rows], x_send.at[1], wr_sem.at[f], left).wait_recv()
            remote(w_right.at[rows], w_far.at[rows], x_send.at[3], wf_sem.at[f], left).start()

    def chunk_here(f):
        rows = pl.ds(f * CHUNK, CHUNK)
        if f % 2 == 1:
            remote(w_left.at[rows], w_left.at[rows], x_send.at[0], wl_sem.at[f], right).wait_recv()
        else:
            remote(w_right.at[rows], w_right.at[rows], x_send.at[1], wr_sem.at[f], left).wait_recv()
        remote(w_far.at[rows], w_far.at[rows], x_send.at[2], wf_sem.at[f], right).wait_recv()

    def product(f, n):
        rows = pl.ds(pl.multiple_of(f * CHUNK, CHUNK), CHUNK)
        to_y = (y + jnp.where(n == 3, 0, jnp.where(n == 0, 2, jnp.where(n == 1, 1, 3)))) % 4
        tokens = pl.ds(pl.multiple_of(to_y * 256, 256), 256)

        def part(index, ref):
            return lax.dot_general(
                cots[index, tokens, :], ref[rows, :], (((1,), (1,)), ((), ())),
                preferred_element_type=F32,
            )

        total = part(x, w_own)
        total = total + part((x + 3) % 4, w_left)
        total = total + part((x + 1) % 4, w_right)
        return to_y, total + part((x + 2) % 4, w_far)

    def to_row(f, n):
        to_y, total = product(f, n)
        most = jnp.max(jnp.max(jnp.abs(total), axis=0, keepdims=True), axis=1, keepdims=True)
        most = jnp.maximum(most, 1e-30)
        sent[f, n] = jnp.round(total * (32000.0 / most)).astype(jnp.int32).astype(jnp.int16)
        steps[f, n] = jnp.broadcast_to(most * (1.0 / 32000.0), (1, 128))
        remote(steps.at[f, n], got_steps.at[f, n], s_send, s_recv.at[f], dev(x, to_y, z, c)).start()
        remote(sent.at[f, n], got.at[f, n], d_send, d_recv.at[f], dev(x, to_y, z, c)).start()

    lane_row = lax.broadcasted_iota(jnp.int32, (128, 128), 1)
    lane_col = lax.broadcasted_iota(jnp.int32, (128, 128), 0)

    def low_tables(first, last):
        for s in range(first, last):
            rows = jnp.concatenate(
                [ang[core, :, s, a * 128 : (a + 1) * 128] for a in range(4) for core in range(2)], axis=0
            )
            for b in range(2):
                pick = jnp.where(lane_col == b * 64 + squeezed(lane_row, s), 1.0, 0.0)
                theta = jnp.dot(rows, pick, precision=lax.Precision.HIGHEST, preferred_element_type=F32)
                sine, cosine = sine_cosine(theta)
                upper = (lax.broadcasted_iota(jnp.int32, theta.shape, 1) & (1 << s)) != 0
                signed = jnp.where(upper, sine, -sine)
                for a in range(4):
                    cos_t[s, 2 * a + b] = cosine[a * 16 : (a + 1) * 16]
                    sin_t[s, 2 * a + b] = signed[a * 16 : (a + 1) * 16]

    def high_tables():
        for s in range(7, 14):
            for a in range(4):
                for core in range(2):
                    sine, cosine = sine_cosine(ang[core, :, s, a * 128 : (a + 1) * 128])
                    cos_t[s, a, core * 8 : core * 8 + 8] = cosine
                    sin_t[s, a, core * 8 : core * 8 + 8] = sine

    pass_on(1, 0)
    pass_on(2, 0)

    @pl.when(is_source)
    def _():
        send_own(3)

    pass_on(1, 1)
    forward(0)
    forward(1)
    pass_on(3, 0)
    remote(ang.at[0, 0:7], ang.at[0, 0:7], g_send, g_recv, sibling).wait_recv()
    remote(ang.at[c], ang.at[c], h_send, h_recv, sibling).start()
    send_codes(2)
    pass_on(2, 1)
    send_codes(3)
    pass_on(4, 0)
    pass_on(1, 2)
    remote(ang.at[0], ang.at[0], h_send, h_recv, sibling).wait_recv()
    pass_on(3, 1)
    loads[3].wait()
    loads[4].wait()
    own_copy.wait()
    pass_on(2, 2)
    group_here(0)
    chunk_here(0)
    to_row(0, 0)
    pass_on(4, 1)
    chunk_here(1)
    to_row(1, 0)
    pass_on(1, 3)
    low_tables(0, 2)
    pass_on(3, 2)
    group_here(1)

    @pl.loop(0, 2)
    def _(f):
        to_row(f, 1)

    forward(2)
    pass_on(2, 3)
    forward(3)
    low_tables(2, 4)
    pass_on(4, 2)
    pass_on(3, 3)
    group_here(2)

    @pl.loop(0, 2)
    def _(f):
        to_row(f, 2)

    chunk_here(2)

    @pl.loop(0, 3)
    def _(n):
        to_row(2, n)

    pass_on(4, 3)
    low_tables(4, 7)
    chunk_here(3)

    @pl.loop(0, 3)
    def _(n):
        to_row(3, n)

    high_tables()
    send_activations()
    group_here(3)

    def finish(f):
        lanes = pl.ds(pl.multiple_of(f * CHUNK, CHUNK), CHUNK)
        remote(steps.at[f], got_steps.at[f], s_send, s_recv.at[f], sibling).wait_recv()
        remote(got.at[f], got.at[f], d_send, d_recv.at[f], sibling).wait_recv()
        place_in_word = lax.broadcasted_iota(jnp.int32, (16, CHUNK), 0)

        def masked(w):
            rows = pl.ds(pl.multiple_of(w * 16, 16), 16)
            total = whole[f, rows, :]
            for j in range(3):
                step = jnp.concatenate([got_steps[f, j], got_steps[f, j]], axis=1)
                total = total + got[f, j, rows, :].astype(jnp.int32).astype(F32) * step
            word = jnp.broadcast_to(clip_v[pl.ds(w, 1), lanes], (16, CHUNK))
            bit = jnp.bitwise_and(jnp.right_shift(word, place_in_word), 1)
            return rows, jnp.where(bit == 1, total, 0.0)

        @pl.loop(1, 16)
        def _(i):
            to = (k + i) % 16
            rows, value = masked(to)
            narrow[f, rows, :] = value.astype(BF16)
            remote(
                narrow.at[f, rows, :], q_in.at[mine16, lanes], e_send, e_recv, (d, to)
            ).start()

        _, value = masked(k)
        q_in[mine16, lanes] = value.astype(BF16)

    @pl.loop(0, CHUNKS)
    def _(f):
        _, total = product(f, 3)
        whole[f] = total
        finish(f)

    remote(a_in.at[0:240], a_in.at[0:240], f_send, f_recv, sibling).wait()

    def row(table, s, tile, index):
        return jnp.broadcast_to(table[s, tile, pl.ds(index, 1), :], (16, 128))

    @pl.loop(0, 16)
    def _(kk):
        rows = pl.ds(pl.multiple_of(kk * 16, 16), 16)
        field = [a_in[rows, t * 128 : (t + 1) * 128].astype(F32) for t in range(8)]
        for s in range(7):
            for t in range(8):
                field[t] = row(cos_t, s, t, kk) * field[t] + row(sin_t, s, t, kk) * lane_partner(field[t], s)
                states[s, rows, t * 128 : (t + 1) * 128] = field[t]
        for s in range(7, 10):
            b = s - 7
            for a in range(4):
                lo = ((a >> b) << (b + 1)) | (a & ((1 << b) - 1))
                hi = lo + (1 << b)
                cosine, sine = row(cos_t, s, a, kk), row(sin_t, s, a, kk)
                field[lo], field[hi] = (
                    cosine * field[lo] - sine * field[hi],
                    sine * field[lo] + cosine * field[hi],
                )
            for t in range(8):
                states[s, rows, t * 128 : (t + 1) * 128] = field[t]

    def fixed_row(table, s, t, m):
        return jnp.broadcast_to(table[s, t % 4, pl.ds((t // 4) * 8 + m, 1), :], (16, 128))

    def halves(lo, hi):
        yield slice(lo * 16, lo * 16 + 16), slice(hi * 16, hi * 16 + 16)

    @pl.loop(0, 8)
    def _(t):
        lanes = pl.ds(pl.multiple_of(t * 128, 128), 128)
        for s in range(10, 14):
            for m, lo, hi in pairs_of(s):
                cosine, sine = fixed_row(cos_t, s, t, m), fixed_row(sin_t, s, t, m)
                for lo_rows, hi_rows in halves(lo, hi):
                    v_lo, v_hi = states[s - 1, lo_rows, lanes], states[s - 1, hi_rows, lanes]
                    states[s, lo_rows, lanes] = cosine * v_lo - sine * v_hi
                    states[s, hi_rows, lanes] = sine * v_lo + cosine * v_hi

    remote(q_in.at[0:240], q_in.at[0:240], e_send, e_recv, sibling).wait()

    def to_section_owner(s):
        @pl.when(d != s)
        def _():
            remote(parts.at[s], by_tokens.at[d], p_send, p_recv, (s, k)).start()

        @pl.when(d == s)
        def _():
            by_tokens[d] = parts[s]

    @pl.loop(0, 8)
    def _(t):
        lanes = pl.ds(pl.multiple_of(t * 128, 128), 128)
        for s in (13, 12, 11, 10):
            source = q_in if s == 13 else tall
            for m, lo, hi in pairs_of(s):
                cosine, sine = fixed_row(cos_t, s, t, m), fixed_row(sin_t, s, t, m)
                total = None
                for lo_rows, hi_rows in halves(lo, hi):
                    q_lo, q_hi = source[lo_rows, lanes].astype(F32), source[hi_rows, lanes].astype(F32)
                    term = q_hi * states[s, lo_rows, lanes] - q_lo * states[s, hi_rows, lanes]
                    total = term if total is None else total + term
                    tall[lo_rows, lanes] = cosine * q_lo + sine * q_hi
                    tall[hi_rows, lanes] = cosine * q_hi - sine * q_lo
                tops[s - 7, t % 4, pl.ds((t // 4) * 8 + m, 1), :] = jnp.sum(total, axis=0, keepdims=True)

    def laid_out(first, last):
        for s in range(first, last):
            for a in range(4):
                parts[s, :, a * 128 : (a + 1) * 128] = tops[s - 7, a]

    laid_out(10, 14)

    @pl.loop(0, 4)
    def _(i):
        to_section_owner(10 + (d + i) % 4)

    @pl.loop(0, 16)
    def _(i):
        kk = (slot + 1 + i) % 16
        rows = pl.ds(pl.multiple_of(kk * 16, 16), 16)
        grad = [tall[rows, t * 128 : (t + 1) * 128] for t in range(8)]
        for s in (9, 8, 7):
            b = s - 7
            for a in range(4):
                lo = ((a >> b) << (b + 1)) | (a & ((1 << b) - 1))
                hi = lo + (1 << b)
                cosine, sine = row(cos_t, s, a, kk), row(sin_t, s, a, kk)
                term = grad[hi] * states[s, rows, lo * 128 : (lo + 1) * 128]
                term = term - grad[lo] * states[s, rows, hi * 128 : (hi + 1) * 128]
                tops[s - 7, a, pl.ds(kk, 1), :] = jnp.sum(term, axis=0, keepdims=True)
                grad[lo], grad[hi] = (
                    cosine * grad[lo] + sine * grad[hi],
                    cosine * grad[hi] - sine * grad[lo],
                )
        for s in (6, 5, 4, 3, 2, 1, 0):
            for t in range(8):
                other = lane_partner(grad[t], s)
                term = other * states[s, rows, t * 128 : (t + 1) * 128]
                terms[s, t, pl.ds(kk, 1), :] = jnp.sum(term, axis=0, keepdims=True)
                grad[t] = row(cos_t, s, t, kk) * grad[t] - row(sin_t, s, t, kk) * other
        for t in range(8):
            q_back[rows, t * 128 : (t + 1) * 128] = grad[t].astype(BF16)

        @pl.when(i < 15)
        def _():
            to = (kk % 8) * 2 + kk // 8
            remote(q_back.at[rows, :], out.at[own16, :], o_send, o_recv, (d, to)).start()

        @pl.when(i == 15)
        def _():
            out[own16, :] = q_back[rows, :]

    laid_out(7, 10)
    for s in range(7):
        sign = jnp.where((lane_col & (1 << s)) == 0, 1.0, -1.0)
        total = None
        for b in range(2):
            pick = jnp.where(lane_row == b * 64 + squeezed(lane_col, s), sign, 0.0)
            rows = jnp.concatenate([terms[s, 2 * a + b] for a in range(4)], axis=0)
            pick = pick.astype(BF16)
            for _ in range(3):
                high = rows.astype(BF16)
                part = jnp.dot(high, pick, preferred_element_type=F32)
                total = part if total is None else total + part
                rows = rows - high.astype(F32)
        for a in range(4):
            parts[s, :, a * 128 : (a + 1) * 128] = total[a * 16 : (a + 1) * 16]

    @pl.loop(0, 10)
    def _(i):
        to_section_owner((d + i) % 10)

    @pl.when(d < 14)
    def _():
        remote(by_tokens.at[0:15], by_tokens.at[0:15], p_send, p_recv, sibling).wait_recv()
        total = by_tokens[0]
        for i in range(1, 16):
            total = total + by_tokens[i]
        for j in range(16):
            row_out[j] = total[j : j + 1, :]

        @pl.loop(1, 16)
        def _(i):
            other = (slot + i) % 16
            remote(
                row_out.at[other], by_width.at[slot], r_send, r_recv, (d, (other % 8) * 2 + other // 8)
            ).start()

        by_width[slot] = row_out[slot]
        remote(by_width.at[0:15], by_width.at[0:15], r_send, r_recv, sibling).wait_recv()
        total = by_width[0]
        for i in range(1, 16):
            total = total + by_width[i]
        final[d] = total

        @pl.loop(1, 16)
        def _(i):
            remote(final.at[d], final.at[d], t_send, t_recv, ((d + i) % 16, k)).start()

        remote(final.at[0:13], final.at[0:13], t_send, t_recv, sibling).wait_recv()
        remote(by_tokens.at[0:13], by_tokens.at[0:13], p_send, p_recv, sibling).wait_send()
        remote(by_width.at[0:15], by_width.at[0:15], r_send, r_recv, sibling).wait_send()
        remote(final.at[0:15], final.at[0:15], t_send, t_recv, sibling).wait_send()

    @pl.when(d >= 14)
    def _():
        remote(final.at[0:14], final.at[0:14], t_send, t_recv, sibling).wait_recv()
        remote(by_tokens.at[0:14], by_tokens.at[0:14], p_send, p_recv, sibling).wait_send()

    for s in range(14):
        angle_out[s : s + 1, :] = final[s]

    remote(q_back.at[0:240], out.at[0:240], o_send, o_recv, sibling).wait()
    remote(ang.at[0, 0:7], ang.at[0, 0:7], g_send, g_recv, sibling).wait_send()
    remote(ang.at[0], ang.at[0], h_send, h_recv, sibling).wait_send()
    remote(steps, got_steps, s_send, s_recv.at[0], sibling).wait_send()
    remote(sent, got, d_send, d_recv.at[0], sibling).wait_send()
    remote(w_own, w_left, x_send.at[0], wl_sem.at[0], right).wait_send()
    remote(w_own, w_right, x_send.at[1], wr_sem.at[0], left).wait_send()
    half_rows = pl.ds(0, 512)
    remote(w_left.at[half_rows], w_far.at[half_rows], x_send.at[2], wf_sem.at[0], right).wait_send()
    remote(w_left.at[half_rows], w_far.at[half_rows], x_send.at[3], wf_sem.at[0], left).wait_send()
    for half in range(2):
        @pl.when(jnp.logical_not(jnp.logical_and(owner_y == y, c == half)))
        def _():
            ref = scaled.at[pl.ds(half * 128, 128), :]
            remote(ref, ref, b_send.at[half], b_recv.at[0], sibling).wait_send()
    for way in range(2):
        @pl.when(is_source)
        def _():
            ref = cots.at[0, 0:512, :]
            remote(ref, ref, z_send.at[way], sib_sem.at[0], sibling).wait_send()
            own_copies(3)[way].wait_send()

        @pl.when(jnp.logical_not(is_source))
        def _():
            ref = cots.at[0, 0:768, :]
            remote(ref, ref, z_send.at[way], sib_sem.at[0], sibling).wait_send()
    remote(cots.at[0:2], cots.at[0:2], z_send.at[2], sib_sem.at[0], sibling).wait_send()


VMEM = pl.BlockSpec(memory_space=pltpu.VMEM)
HBM = pl.BlockSpec(memory_space=pltpu.HBM)


def body(activations, angles, clip_bits, codes, exponents, cotangent):
    dma = pltpu.SemaphoreType.DMA
    return pl.pallas_call(
        all_kernel,
        out_shape=(
            jax.ShapeDtypeStruct((256, 1024), BF16),
            jax.ShapeDtypeStruct((14, 512), F32),
        ),
        in_specs=[HBM] * 6,
        out_specs=(VMEM,) * 2,
        scratch_shapes=[
            pltpu.VMEM((16, 1024), jnp.int32),
            pltpu.VMEM((1, 640), jnp.int32),
            pltpu.VMEM((256, 640), BF16),
            pltpu.VMEM((14, 512), F32),
            pltpu.VMEM((1024, 640), BF16),
            pltpu.VMEM((256, 640), BF16),
            pltpu.VMEM((4, 1024, 640), BF16),
            pltpu.VMEM((1024, 640), BF16),
            pltpu.VMEM((1024, 640), BF16),
            pltpu.VMEM((1024, 640), BF16),
            pltpu.VMEM((CHUNKS, 3, 256, CHUNK), jnp.int16),
            pltpu.VMEM((CHUNKS, 3, 256, CHUNK), jnp.int16),
            pltpu.VMEM((CHUNKS, 3, 1, 128), F32),
            pltpu.VMEM((CHUNKS, 3, 1, 128), F32),
            pltpu.VMEM((CHUNKS, 256, CHUNK), F32),
            pltpu.VMEM((CHUNKS, 256, CHUNK), BF16),
            pltpu.VMEM((256, 1024), BF16),
            pltpu.VMEM((256, 1024), BF16),
            pltpu.VMEM((2, 8, 16, 512), F32),
            pltpu.VMEM((14, 8, 16, 128), F32),
            pltpu.VMEM((14, 8, 16, 128), F32),
            pltpu.VMEM((14, 256, 1024), F32),
            pltpu.VMEM((7, 8, 16, 128), F32),
            pltpu.VMEM((7, 4, 16, 128), F32),
            pltpu.VMEM((256, 1024), F32),
            pltpu.VMEM((256, 1024), BF16),
            pltpu.VMEM((14, 16, 512), F32),
            pltpu.VMEM((16, 16, 512), F32),
            pltpu.VMEM((16, 1, 512), F32),
            pltpu.VMEM((16, 1, 512), F32),
            pltpu.VMEM((16, 1, 512), F32),
            dma((6,)), dma((4,)), dma((CHUNKS,)), dma((CHUNKS,)), dma((CHUNKS,)),
            dma((2,)), dma((4,)), dma((2, 4)), dma((3,)), dma((4, 4)), dma((4, 4)), dma((4,)),
            dma, dma((CHUNKS,)), dma, dma((CHUNKS,)), dma, dma, dma, dma, dma, dma, dma, dma,
            dma, dma, dma, dma, dma, dma, dma, dma,
        ],
        compiler_params=pltpu.CompilerParams(
            collective_id=0, has_side_effects=True, vmem_limit_bytes=56 * 2**20
        ),
        cost_estimate=pl.CostEstimate(flops=5400000000, bytes_accessed=6000000, transcendentals=0),
    )(activations, clip_bits, codes, exponents[None, :], cotangent, angles)


def solution(mesh):
    placed = (
        P("dp", "tensor"),
        P(None, "tensor"),
        P("dp", "tensor"),
        P("tensor", "dp"),
        P(),
        P("dp", "tensor"),
    )
    return jax.shard_map(
        body,
        mesh=mesh,
        in_specs=placed,
        out_specs=(P("dp", "tensor"), P(None, "tensor")),
        check_vma=False,
    )
```
